128 devices in a mesh: idx: 64 (over y, x, z), enc: 2 (over core).
Axes of the slice: x: 4, y: 4, z: 4, core: 2. Of those that a mesh axis runs over, the one named last changes fastest.
Arguments:
- queries: bfloat16 [262144, 1024], P(('idx', 'enc')), may hold values from -12 to 12
- positives: bfloat16 [262144, 1024], P(('idx', 'enc')), may hold values from -6 to 6
- passages: bfloat16 [131072, 1024], P('idx'), may hold values from -12 to 12
- negatives: int32 [128, 2048], P(('idx', 'enc')), may hold values from -1 to 131071, as said below
Outputs:
- query_loss: float32 [262144], P(('idx', 'enc'))
- grad_queries: bfloat16 [262144, 1024], P(('idx', 'enc'))
- grad_passages: bfloat16 [131072, 1024], P('idx')
The draws below stay inside these ranges and needn't reach their ends.
Inputs may be any that keep to these rules, and one draw needn't show every extreme that they name: `negatives`: -1 marks a padding slot. Of the 2048 slots of one device (its 1 row), at most 32 name passages of one index shard (ids 2048 * k to 2048 * k + 2047), and in every draw some shard is named exactly 32 times by every device.
All inputs are finite; a program needn't handle non-finite values.
Results may differ from the reference program's by a relative error of at most 0.0055.
Values may be sent and summed in bfloat16 or wider, within the bound.
A program may use at most 128 MiB of HBM per device.

```python
import math
import jax
import jax.numpy as jnp
from jax import lax

D = 1024
GQ = 2048
ROWS_SHARD = 2048
LSCALE = 32
NEG = 2048
LIST_DEV = 2048
CAP = 32
TRAINERS = 128
GROUPS = 128
QTOT = 262144
PASSAGES = 131072
N_IDX = 64


def draw_queries(key, part):
    key = jax.random.fold_in(key, 11)
    values = jax.random.truncated_normal(key, -6.0, 6.0, (QTOT, D), jnp.float32)
    return values.astype(jnp.bfloat16)


def draw_passages(key, part):
    key = jax.random.fold_in(key, 23)
    values = jax.random.truncated_normal(key, -6.0, 6.0, (PASSAGES, D), jnp.float32)
    return values.astype(jnp.bfloat16)


def draw_negatives(key, part):
    key = jax.random.fold_in(key, 37)
    key_hot, key_first, key_count, key_row, key_perm = jax.random.split(key, 5)
    owners = jnp.arange(N_IDX, dtype=jnp.int32)
    first_hot = jax.random.randint(key_first, (), 0, N_IDX, dtype=jnp.int32)
    hot_owner = (jax.random.randint(key_hot, (N_IDX,), 0, 4, dtype=jnp.int32) == 0) | (owners == first_hot)
    light = jax.random.randint(key_count, (TRAINERS, N_IDX), CAP // 4, CAP // 2 + 1, dtype=jnp.int32)
    counts = jnp.where(hot_owner[None, :], CAP, light)
    bounds = jnp.cumsum(counts, axis=1)
    slot_index = jnp.arange(LIST_DEV, dtype=jnp.int32)
    owner_of = jnp.sum((slot_index[None, :, None] >= bounds[:, None, :]).astype(jnp.int32), axis=2)
    is_live = owner_of < N_IDX
    local_row = jax.random.randint(key_row, (TRAINERS, LIST_DEV), 0, ROWS_SHARD, dtype=jnp.int32)
    slot_ids = jnp.where(is_live, owner_of * ROWS_SHARD + local_row, -1)
    perm_keys = jax.random.split(key_perm, TRAINERS)
    shuffled = jax.vmap(lambda one_key, one_row: jax.random.permutation(one_key, one_row))(perm_keys, slot_ids)
    return shuffled.reshape(GROUPS, NEG).astype(jnp.int32)


def level_of(own_key, dims, cuts, low, high):
    def one(axis_at, shards_of):
        heights = jax.random.uniform(jax.random.fold_in(jax.random.fold_in(own_key, 6), axis_at), (shards_of,), jnp.float32, low / len(cuts), high / len(cuts))
        return jnp.repeat(jnp.exp(heights), dims[axis_at] // shards_of).reshape((-1,) + (1,) * (len(dims) - axis_at - 1))

    factor_of = one(*cuts[0])
    for cut in cuts[1:]:
        factor_of = factor_of * one(*cut)
    return factor_of


def gaussian(own_key, dims, width, most, cuts=(), held_as=jnp.bfloat16):
    loudness = level_of(own_key, dims, cuts, -0.22, 0.18) if cuts else 1.0
    values = jax.random.normal(own_key, dims, jnp.float32) * width * loudness
    return jnp.minimum(jnp.maximum(values, -most), most).astype(held_as)


def setup_inputs(seed: int = 0) -> dict:
    streams_of = jax.random.split(jax.random.key(seed), 5)
    queries = draw_queries(jax.random.fold_in(streams_of[4], 71), 0)
    positives = gaussian(streams_of[1], (QTOT, D), 1.0, 6.0, ((0, 128),))
    passages = draw_passages(jax.random.fold_in(streams_of[4], 71), 0)
    negatives = draw_negatives(jax.random.fold_in(streams_of[4], 71), 0)
    return {"queries": queries, "positives": positives, "passages": passages, "negatives": negatives}


masked_value = -1e+30

def group_terms(query_block, positive_block, neg_rows, is_live, loss_scale):
    feature_dim = query_block.shape[1]
    logit_scale = 3.0 / math.sqrt(feature_dim)
    pos_logit = logit_scale * lax.optimization_barrier(jnp.sum(query_block.astype(jnp.float32) * positive_block.astype(jnp.float32), axis=1))
    neg_logit = logit_scale * lax.dot_general(query_block, neg_rows, (((1,), (1,)), ((), ())), preferred_element_type=jnp.float32)
    masked = jnp.where(is_live[None, :], neg_logit, masked_value)
    top_logit = jnp.maximum(lax.optimization_barrier(jnp.max(masked, axis=1)), pos_logit)
    neg_exp = jnp.where(is_live[None, :], jnp.exp(masked - top_logit[:, None]), 0.0)
    pos_exp = jnp.exp(pos_logit - top_logit)
    norm_total = pos_exp + lax.optimization_barrier(jnp.sum(neg_exp, axis=1))
    query_loss = top_logit + jnp.log(norm_total) - pos_logit
    factor = loss_scale * logit_scale
    weights = (factor * neg_exp / norm_total[:, None]).astype(jnp.bfloat16)
    grad_query = jnp.dot(weights, neg_rows, preferred_element_type=jnp.float32)
    grad_query = grad_query + (factor * (pos_exp / norm_total - 1.0))[:, None] * positive_block.astype(jnp.float32)
    row_grad = lax.dot_general(weights, query_block, (((0,), (0,)), ((), ())), preferred_element_type=jnp.float32).astype(jnp.bfloat16)
    return (query_loss, grad_query.astype(jnp.bfloat16), row_grad)

def reference(queries, positives, passages, negatives):
    feature_dim = queries.shape[1]
    group_count = negatives.shape[0]
    query_groups = queries.reshape(group_count, GQ, feature_dim)
    positive_groups = positives.reshape(group_count, GQ, feature_dim)

    def one_group(grad_sum, group_inputs):
        query_block, positive_block, group_ids = group_inputs
        is_live = group_ids >= 0
        neg_rows = jnp.take(passages, jnp.maximum(group_ids, 0).astype(jnp.int32), axis=0)
        query_loss, grad_query, row_grad = group_terms(query_block, positive_block, neg_rows, is_live, LSCALE)
        target = jnp.where(is_live, group_ids, PASSAGES).astype(jnp.int32)
        grad_sum = grad_sum.at[target].add(row_grad.astype(jnp.float32), mode='drop')
        return (grad_sum, (query_loss, grad_query))
    grad_sum, (losses, grads) = lax.scan(one_group, jnp.zeros((PASSAGES, feature_dim), jnp.float32), (query_groups, positive_groups, negatives))
    return (losses.reshape(QTOT), grads.reshape(QTOT, feature_dim), grad_sum.astype(jnp.bfloat16))
```

```python
import functools
import math

import jax
import jax.numpy as jnp
from jax import lax
from jax.experimental import pallas as pl
from jax.experimental.pallas import tpu as pltpu
from jax.sharding import PartitionSpec as P

LSCALE = 32
CAP = 32
LANES = 128
MESH = pl.DeviceIdType.MESH
NONE = -1e30


def flip(u, v):
    if isinstance(u, int):
        return 1 - v if u else v
    return u + v - 2 * u * v


def place_bits(c, j, n, group):
    low = int(math.log2(group))
    count = int(math.log2(n))
    p = [(j >> k) & 1 for k in range(low)]
    p += [lax.rem(lax.div(c, 1 << k), 2) for k in range(count - low)]
    if n != 64:
        return p
    t0, t1, b0, b1, a0, a1 = p
    return [t0, t1, flip(t0, a0), flip(t1, a1), flip(t0, b0), flip(t1, b1)]


def place_of(distance, n):
    if n != 64:
        return distance
    z, x, y = distance & 3, (distance >> 2) & 3, (distance >> 4) & 3
    return ((x ^ z) << 4) + ((y ^ z) << 2) + z


def iota(shape, dim):
    return lax.broadcasted_iota(jnp.int32, shape, dim)


def dot(a, b, dims=((1,), (0,))):
    return lax.dot_general(a, b, (dims, ((), ())), preferred_element_type=jnp.float32)


def turned(rows):
    m = rows.shape[0]
    if m < LANES:
        rows = jnp.concatenate([rows, jnp.zeros((LANES - m, LANES), rows.dtype)], axis=0)
    return rows.T


def request_table(ids, me, n, shard_rows):
    slots = ids.shape[1]
    shift = int(math.log2(shard_rows))
    live = ids >= 0
    place = place_of(jnp.bitwise_xor(lax.shift_right_arithmetic(ids, shift), me), n)
    place = jnp.where(live, place, -1)
    row = jnp.bitwise_and(ids, shard_rows - 1) + 1
    hot = iota((n, slots), 0) == place
    hot_f = jnp.where(hot, 1.0, 0.0)
    width = min(256, slots)
    before = jnp.where(
        iota((width, width), 0) < iota((width, width), 1), 1.0, 0.0
    ).astype(jnp.bfloat16)
    carry = jnp.zeros((n, 1), jnp.float32)
    ranks = []
    for at in range(0, slots, width):
        part = hot_f[:, at : at + width]
        ahead = dot(part.astype(jnp.bfloat16), before) + carry
        ranks.append(jnp.sum(part * ahead, axis=0, keepdims=True))
        carry = carry + jnp.sum(part, axis=1, keepdims=True)
    rank = jnp.concatenate(ranks, axis=1).astype(jnp.int32)
    of_rank = jnp.where(iota((LANES, slots), 0) == rank, 1.0, 0.0).astype(jnp.bfloat16)
    high = lax.shift_right_arithmetic(row, 6).astype(jnp.float32)
    low = jnp.bitwise_and(row, 63).astype(jnp.float32)
    values = jnp.concatenate([hot_f * high, hot_f * low], axis=0).astype(jnp.bfloat16)
    table = dot(values, of_rank, ((1,), (1,)))
    return (table[:n] * 64.0 + table[n:]).astype(jnp.int32) - 1


def slot_row(table, n):
    slots = n * CAP
    shifted = table + 1
    high = lax.shift_right_arithmetic(shifted, 6).astype(jnp.float32)
    low = jnp.bitwise_and(shifted, 63).astype(jnp.float32)
    parts = jnp.concatenate([high, low], axis=0).astype(jnp.bfloat16)
    lane = jnp.bitwise_and(iota((LANES, slots), 1), CAP - 1)
    spread = jnp.where(iota((LANES, slots), 0) == lane, 1.0, 0.0).astype(jnp.bfloat16)
    wide = dot(parts, spread)
    both = wide[:n] * 64.0 + wide[n:]
    mine = lax.shift_right_arithmetic(iota((n, slots), 1), 5) == iota((n, slots), 0)
    row = jnp.sum(jnp.where(mine, both, 0.0), axis=0, keepdims=True)
    return row.astype(jnp.int32) - 1


def kernel(
    n, group,
    ids_ref, q_hbm, pos_hbm, pas_hbm,
    loss_ref, gq_hbm, gp_hbm,
    q, pos, pas, send, got, ret, big, wt,
    req, want, wcol, bias, wrow, tops, sums, prow, crow,
    load_s, rq_s, rq_r, f_s, f_r, r_s, r_r, fw_s, fw_r, wx_s, wx_r, oq_s, op_s,
):
    me, core = lax.axis_index("idx"), lax.axis_index("enc")
    queries, depth = q.shape
    shard_rows = pas.shape[0]
    slots = n * CAP
    chunk = group * CAP
    chunks = n // group
    scale = 3.0 / math.sqrt(depth)
    factor = LSCALE * scale
    steps = [
        (1 << k) * (1 - 2 * lax.rem(lax.div(me, 1 << k), 2))
        for k in range(int(math.log2(n)))
    ]

    def partner(c, j):
        bits = place_bits(c, j, n, group)
        there = me
        for bit, step in zip(bits, steps):
            if isinstance(bit, int):
                there = there + step if bit else there
            else:
                there = there + bit * step
        return there

    def each(work):
        def body(c, carry):
            for j in range(group):
                p = c * group + j
                if j == 0:
                    @pl.when(c > 0)
                    def _():
                        work(p, partner(c, 0))
                else:
                    work(p, partner(c, j))
            return carry

        lax.fori_loop(0, chunks, body, 0)

    def of_chunk(c, work):
        for j in range(group):
            p = c * group + j
            if j == 0:
                @pl.when(c > 0)
                def _():
                    work(p, partner(c, 0))
            else:
                work(p, partner(c, j))

    def part(c):
        return pl.ds(pl.multiple_of(c * chunk, chunk), chunk)

    def rows_at(p):
        return pl.ds(pl.multiple_of(p * CAP, CAP), CAP)

    def ask(p, there):
        return pltpu.make_async_remote_copy(
            src_ref=req.at[p], dst_ref=want.at[p], send_sem=rq_s.at[p],
            recv_sem=rq_r.at[p], device_id=(there, core), device_id_type=MESH)

    def fetch(p, there):
        return pltpu.make_async_remote_copy(
            src_ref=send.at[rows_at(p)], dst_ref=got.at[rows_at(p)], send_sem=f_s.at[p],
            recv_sem=f_r.at[p], device_id=(there, core), device_id_type=MESH)

    def give(p, there):
        return pltpu.make_async_remote_copy(
            src_ref=send.at[rows_at(p)], dst_ref=ret.at[core, rows_at(p)], send_sem=r_s.at[p],
            recv_sem=r_r.at[p], device_id=(there, core), device_id_type=MESH)

    def pass_on(c, whose):
        return pltpu.make_async_remote_copy(
            src_ref=ret.at[whose, part(c)], dst_ref=ret.at[whose, part(c)],
            send_sem=fw_s.at[c], recv_sem=fw_r.at[c],
            device_id=(me, 1 - core), device_id_type=MESH)

    def pass_row(whose):
        return pltpu.make_async_remote_copy(
            src_ref=wrow.at[whose], dst_ref=wrow.at[whose], send_sem=wx_s, recv_sem=wx_r,
            device_id=(me, 1 - core), device_id_type=MESH)

    loads = [
        pltpu.make_async_copy(src, dst, load_s.at[k])
        for k, (src, dst) in enumerate([(pas_hbm, pas), (q_hbm, q), (pos_hbm, pos)])
    ]

    barrier = pltpu.get_barrier_semaphore()
    each(lambda p, there: pl.semaphore_signal(
        barrier, inc=1, device_id=(there, core), device_id_type=MESH))
    pl.semaphore_signal(barrier, inc=1, device_id=(me, 1 - core), device_id_type=MESH)
    for load in loads:
        load.start()
    table = request_table(ids_ref[...], me, n, shard_rows)
    for p in range(n):
        req[p] = table[p : p + 1]
    want[0] = table[0:1]
    pl.semaphore_wait(barrier, n)

    each(lambda p, there: ask(p, there).start())
    each(lambda p, there: ask(p, there).wait_recv())
    wanted = want[:, 0, :]
    wanted_t = turned(wanted)
    for p in range(n):
        wcol[p * CAP : (p + 1) * CAP, :] = jnp.broadcast_to(
            wanted_t[:CAP, p : p + 1], (CAP, LANES))

    loads[0].wait()

    def gather(c, carry):
        w = wcol[part(c), :]
        lane = iota((chunk, LANES), 1)
        hot = jnp.concatenate(
            [jnp.where(w == lane + k, 1.0, 0.0).astype(jnp.bfloat16)
             for k in range(0, shard_rows, LANES)], axis=1)
        send[part(c), :] = dot(hot, pas[...]).astype(jnp.bfloat16)
        of_chunk(c, lambda p, there: fetch(p, there).start())
        return carry

    lax.fori_loop(0, chunks, gather, 0)
    got[0:CAP, :] = send[0:CAP, :]

    wrow[core] = slot_row(wanted, n)
    pass_row(core).start()
    asked_t = turned(req[:, 0, :])
    for p in range(n):
        bias[p * CAP : (p + 1) * CAP, :] = jnp.broadcast_to(
            jnp.where(asked_t[:CAP, p : p + 1] >= 0, 0.0, NONE), (CAP, LANES))
    loads[1].wait()
    loads[2].wait()
    block = min(256, queries)

    def block_at(b):
        return pl.ds(pl.multiple_of(b * block, block), block)

    def positive(b, carry):
        both = q[block_at(b), :].astype(jnp.float32) * pos[block_at(b), :].astype(jnp.float32)
        total = both[:, :LANES]
        for k in range(LANES, depth, LANES):
            total = total + both[:, k : k + LANES]
        prow[:, block_at(b)] = scale * jnp.sum(total.T, axis=0, keepdims=True)
        return carry

    lax.fori_loop(0, queries // block, positive, 0)

    wide = min(512, queries)

    def logits(c, carry):
        of_chunk(c, lambda p, there: fetch(p, there).wait_recv())

        def one(b, carry):
            at = pl.ds(pl.multiple_of(b * wide, wide), wide)
            x = scale * dot(got[part(c), :], q[at, :], ((1,), (1,)))
            x = x + jnp.concatenate([bias[part(c), :]] * (wide // LANES), axis=1)
            top = jnp.max(x, axis=0, keepdims=True)
            x = jnp.exp(x - top)
            big[part(c), at] = x
            tops[c, :, at] = top
            sums[c, :, at] = jnp.sum(x, axis=0, keepdims=True)
            return carry

        return lax.fori_loop(0, queries // wide, one, carry)

    lax.fori_loop(0, chunks, logits, 0)

    pos_logit = prow[...]
    top = pos_logit
    for c in range(chunks):
        top = jnp.maximum(top, tops[c])
    pos_exp = jnp.exp(pos_logit - top)
    total = pos_exp
    for c in range(chunks):
        total = total + sums[c] * jnp.exp(tops[c] - top)
    for c in range(chunks):
        tops[c] = jnp.exp(tops[c] - top) * (factor / total)
    crow[...] = factor * (pos_exp / total - 1.0)
    loss_ref[...] = top + jnp.log(total) - pos_logit

    each(lambda p, there: fetch(p, there).wait_send())

    def row_grads(c, carry):
        wt[part(c), :] = (big[part(c), :] * tops[c]).astype(jnp.bfloat16)
        send[part(c), :] = dot(wt[part(c), :], q[...]).astype(jnp.bfloat16)
        of_chunk(c, lambda p, there: give(p, there).start())
        return carry

    lax.fori_loop(0, chunks, row_grads, 0)
    ret[core, 0:CAP, :] = send[0:CAP, :]

    def out_q(b):
        return pltpu.make_async_copy(
            pas.at[block_at(b)], gq_hbm.at[block_at(b)], oq_s.at[b])

    def query_grads(b, carry):
        g = dot(wt[:, block_at(b)], got[...], ((0,), (0,)))
        coef = jnp.broadcast_to(crow[:, block_at(b)], (LANES, block)).T
        coef = jnp.concatenate([coef] * (depth // LANES), axis=1)
        g = g + coef * pos[block_at(b), :].astype(jnp.float32)
        pas[block_at(b), :] = g.astype(jnp.bfloat16)
        out_q(b).start()
        return carry

    lax.fori_loop(0, queries // block, query_grads, 0)

    tall = min(512, shard_rows)

    def tall_at(b):
        return pl.ds(pl.multiple_of(b * tall, tall), tall)

    def clear(b, carry):
        big[tall_at(b), 0:depth] = jnp.zeros((tall, depth), jnp.float32)
        return carry

    lax.fori_loop(0, shard_rows // tall, clear, 0)
    pass_row(1 - core).wait_recv()

    def collect(c, carry):
        @pl.when(c < chunks)
        def _():
            of_chunk(c, lambda p, there: give(p, there).wait_recv())
            pass_on(c, core).start()

        @pl.when(c > 0)
        def _():
            last = c - 1
            pass_on(last, 1 - core).wait_recv()

            def one(b, carry):
                here = iota((tall, chunk), 0) + b * tall
                total = big[tall_at(b), 0:depth]
                for whose in range(2):
                    hot = jnp.where(here == wrow[whose, :, part(last)], 1.0, 0.0)
                    total = total + dot(hot.astype(jnp.bfloat16), ret[whose, part(last), :])
                big[tall_at(b), 0:depth] = total
                return carry

            lax.fori_loop(0, shard_rows // tall, one, 0)

        return carry

    lax.fori_loop(0, chunks + 1, collect, 0)

    def out_p(b):
        return pltpu.make_async_copy(
            got.at[tall_at(b)], gp_hbm.at[tall_at(b)], op_s.at[b])

    def finish(b, carry):
        got[tall_at(b), :] = big[tall_at(b), 0:depth].astype(jnp.bfloat16)
        out_p(b).start()
        return carry

    lax.fori_loop(0, shard_rows // tall, finish, 0)

    each(lambda p, there: ask(p, there).wait_send())
    each(lambda p, there: give(p, there).wait_send())
    pass_row(core).wait_send()

    def close_pass(c, carry):
        pass_on(c, core).wait_send()
        return carry

    lax.fori_loop(0, chunks, close_pass, 0)

    def close_q(b, carry):
        out_q(b).wait()
        return carry

    lax.fori_loop(0, queries // block, close_q, 0)

    def close_p(b, carry):
        out_p(b).wait()
        return carry

    lax.fori_loop(0, shard_rows // tall, close_p, 0)


def local(group, queries, positives, passages, negatives):
    n = lax.axis_size("idx")
    count, depth = queries.shape
    shard_rows = passages.shape[0]
    slots = n * CAP
    chunks = n // group
    block = min(256, count)
    tall = min(512, shard_rows)
    any_space = pl.BlockSpec(memory_space=pl.ANY)
    vmem = pl.BlockSpec(memory_space=pltpu.VMEM)
    dma = pltpu.SemaphoreType.DMA
    bf16, f32 = jnp.bfloat16, jnp.float32
    loss, grad_q, grad_p = pl.pallas_call(
        functools.partial(kernel, n, group),
        out_shape=(
            jax.ShapeDtypeStruct((1, count), f32),
            jax.ShapeDtypeStruct((count, depth), bf16),
            jax.ShapeDtypeStruct((shard_rows, depth), bf16),
        ),
        in_specs=[vmem, any_space, any_space, any_space],
        out_specs=(vmem, any_space, any_space),
        scratch_shapes=[
            pltpu.VMEM((count, depth), bf16),
            pltpu.VMEM((count, depth), bf16),
            pltpu.VMEM((shard_rows, depth), bf16),
            pltpu.VMEM((slots, depth), bf16),
            pltpu.VMEM((slots, depth), bf16),
            pltpu.VMEM((2, slots, depth), bf16),
            pltpu.VMEM((slots, count), f32),
            pltpu.VMEM((slots, count), bf16),
            pltpu.VMEM((n, 1, LANES), jnp.int32),
            pltpu.VMEM((n, 1, LANES), jnp.int32),
            pltpu.VMEM((slots, LANES), jnp.int32),
            pltpu.VMEM((slots, LANES), f32),
            pltpu.VMEM((2, 1, slots), jnp.int32),
            pltpu.VMEM((chunks, 1, count), f32),
            pltpu.VMEM((chunks, 1, count), f32),
            pltpu.VMEM((1, count), f32),
            pltpu.VMEM((1, count), f32),
            dma((3,)),
            dma((n,)), dma((n,)),
            dma((n,)), dma((n,)),
            dma((n,)), dma((n,)),
            dma((chunks,)), dma((chunks,)),
            dma, dma,
            dma((count // block,)),
            dma((shard_rows // tall,)),
        ],
        compiler_params=pltpu.CompilerParams(
            collective_id=0, has_side_effects=True, vmem_limit_bytes=62 << 20
        ),
        cost_estimate=pl.CostEstimate(
            flops=12 * slots * count * depth, bytes_accessed=20 * count * depth,
            transcendentals=slots * count,
        ),
    )(negatives.reshape(1, -1), queries, positives, passages)
    return loss.reshape(-1), grad_q, grad_p


def solution(mesh, group=8):
    placed = (
        P(("idx", "enc"), None),
        P(("idx", "enc"), None),
        P("idx", None),
        P(("idx", "enc"), None),
    )
    return jax.shard_map(
        functools.partial(local, group),
        mesh=mesh,
        in_specs=placed,
        out_specs=(P(("idx", "enc")), P(("idx", "enc"), None), P("idx", None)),
        check_vma=False,
    )
```

```python
import functools
import math

import jax
import jax.numpy as jnp
from jax import lax
from jax.experimental import pallas as pl
from jax.experimental.pallas import tpu as pltpu
from jax.sharding import PartitionSpec as P

LSCALE = 32
CAP = 32
LANES = 128
MESH = pl.DeviceIdType.MESH
NONE = -1e30


def flip(u, v):
    if isinstance(u, int):
        return 1 - v if u else v
    return u + v - 2 * u * v


def place_bits(c, j, n, group):
    low = int(math.log2(group))
    count = int(math.log2(n))
    p = [1 - ((j >> k) & 1) for k in range(low)]
    p += [1 - lax.rem(lax.div(c, 1 << k), 2) for k in range(count - low)]
    if n != 64:
        return p
    t0, t1, b0, b1, a0, a1 = p
    return [t0, t1, flip(t0, a0), flip(t1, a1), flip(t0, b0), flip(t1, b1)]


def place_of(distance, n):
    if n != 64:
        return n - 1 - distance
    z, x, y = distance & 3, (distance >> 2) & 3, (distance >> 4) & 3
    return n - 1 - (((x ^ z) << 4) + ((y ^ z) << 2) + z)


def iota(shape, dim):
    return lax.broadcasted_iota(jnp.int32, shape, dim)


def dot(a, b, dims=((1,), (0,))):
    return lax.dot_general(a, b, (dims, ((), ())), preferred_element_type=jnp.float32)


def turned(rows):
    m = rows.shape[0]
    if m < LANES:
        rows = jnp.concatenate([rows, jnp.zeros((LANES - m, LANES), rows.dtype)], axis=0)
    return rows.T


def request_table(ids, me, n, shard_rows):
    slots = ids.shape[1]
    shift = int(math.log2(shard_rows))
    live = ids >= 0
    place = place_of(jnp.bitwise_xor(lax.shift_right_arithmetic(ids, shift), me), n)
    place = jnp.where(live, place, -1)
    row = jnp.bitwise_and(ids, shard_rows - 1) + 1
    hot = iota((n, slots), 0) == place
    hot_f = jnp.where(hot, 1.0, 0.0)
    width = min(256, slots)
    before = jnp.where(
        iota((width, width), 0) < iota((width, width), 1), 1.0, 0.0
    ).astype(jnp.bfloat16)
    carry = jnp.zeros((n, 1), jnp.float32)
    ranks = []
    for at in range(0, slots, width):
        part = hot_f[:, at : at + width]
        ahead = dot(part.astype(jnp.bfloat16), before) + carry
        ranks.append(jnp.sum(part * ahead, axis=0, keepdims=True))
        carry = carry + jnp.sum(part, axis=1, keepdims=True)
    rank = jnp.concatenate(ranks, axis=1).astype(jnp.int32)
    of_rank = jnp.where(iota((LANES, slots), 0) == rank, 1.0, 0.0).astype(jnp.bfloat16)
    high = lax.shift_right_arithmetic(row, 6).astype(jnp.float32)
    low = jnp.bitwise_and(row, 63).astype(jnp.float32)
    values = jnp.concatenate([hot_f * high, hot_f * low], axis=0).astype(jnp.bfloat16)
    table = dot(values, of_rank, ((1,), (1,)))
    return (table[:n] * 64.0 + table[n:]).astype(jnp.int32) - 1


def slot_row(table, n):
    slots = n * CAP
    shifted = table + 1
    high = lax.shift_right_arithmetic(shifted, 6).astype(jnp.float32)
    low = jnp.bitwise_and(shifted, 63).astype(jnp.float32)
    parts = jnp.concatenate([high, low], axis=0).astype(jnp.bfloat16)
    lane = jnp.bitwise_and(iota((LANES, slots), 1), CAP - 1)
    spread = jnp.where(iota((LANES, slots), 0) == lane, 1.0, 0.0).astype(jnp.bfloat16)
    wide = dot(parts, spread)
    both = wide[:n] * 64.0 + wide[n:]
    mine = lax.shift_right_arithmetic(iota((n, slots), 1), 5) == iota((n, slots), 0)
    row = jnp.sum(jnp.where(mine, both, 0.0), axis=0, keepdims=True)
    return row.astype(jnp.int32) - 1


def kernel(
    n, group,
    ids_ref, q_hbm, pos_hbm, pas_hbm,
    loss_ref, gq_hbm, gp_hbm,
    q, pos, pas, send, got, ret, big, wt,
    req, want, wcol, bias, wrow, tops, sums, prow, crow,
    load_s, rq_s, rq_r, f_s, f_r, r_s, r_r, fw_s, fw_r, wx_s, wx_r, oq_s, op_s,
):
    me, core = lax.axis_index("idx"), lax.axis_index("enc")
    queries, depth = q.shape
    shard_rows = pas.shape[0]
    slots = n * CAP
    chunk = group * CAP
    chunks = n // group
    scale = 3.0 / math.sqrt(depth)
    factor = LSCALE * scale
    steps = [
        (1 << k) * (1 - 2 * lax.rem(lax.div(me, 1 << k), 2))
        for k in range(int(math.log2(n)))
    ]

    def partner(c, j):
        bits = place_bits(c, j, n, group)
        there = me
        for bit, step in zip(bits, steps):
            if isinstance(bit, int):
                there = there + step if bit else there
            else:
                there = there + bit * step
        return there

    def of_chunk(c, work):
        for j in range(group):
            if j == group - 1:
                @pl.when(c < chunks - 1)
                def _():
                    work(c * group + j, partner(c, j))
            else:
                work(c * group + j, partner(c, j))

    def loop(start, stop, body):
        def step(c, carry):
            body(c)
            return carry

        lax.fori_loop(start, stop, step, 0)

    def each(work):
        loop(0, chunks, lambda c: of_chunk(c, work))

    def part(c):
        return pl.ds(pl.multiple_of(c * chunk, chunk), chunk)

    def rows_at(p):
        return pl.ds(pl.multiple_of(p * CAP, CAP), CAP)

    def pair(c):
        return pl.ds(pl.multiple_of(c * 2 * chunk, 2 * chunk), 2 * chunk)

    def half(c, whose):
        return pl.ds(pl.multiple_of((c * 2 + whose) * chunk, chunk), chunk)

    def home(p, whose):
        c, j = lax.div(p, group), lax.rem(p, group)
        return pl.ds(pl.multiple_of((c * 2 + whose) * chunk + j * CAP, CAP), CAP)

    def ask(p, there):
        return pltpu.make_async_remote_copy(
            src_ref=req.at[p], dst_ref=want.at[p], send_sem=rq_s.at[p],
            recv_sem=rq_r.at[p], device_id=(there, core), device_id_type=MESH)

    def fetch(p, there):
        return pltpu.make_async_remote_copy(
            src_ref=send.at[rows_at(p)], dst_ref=got.at[rows_at(p)], send_sem=f_s.at[p],
            recv_sem=f_r.at[p], device_id=(there, core), device_id_type=MESH)

    def give(p, there):
        return pltpu.make_async_remote_copy(
            src_ref=send.at[rows_at(p)], dst_ref=ret.at[home(p, core)], send_sem=r_s.at[p],
            recv_sem=r_r.at[p], device_id=(there, core), device_id_type=MESH)

    def pass_on(c, whose):
        return pltpu.make_async_remote_copy(
            src_ref=ret.at[half(c, whose)], dst_ref=ret.at[half(c, whose)],
            send_sem=fw_s.at[c], recv_sem=fw_r.at[c],
            device_id=(me, 1 - core), device_id_type=MESH)

    def pass_row(whose):
        return pltpu.make_async_remote_copy(
            src_ref=wrow.at[whose], dst_ref=wrow.at[whose], send_sem=wx_s, recv_sem=wx_r,
            device_id=(me, 1 - core), device_id_type=MESH)

    loads = [
        pltpu.make_async_copy(src, dst, load_s.at[k])
        for k, (src, dst) in enumerate([(pas_hbm, pas), (q_hbm, q), (pos_hbm, pos)])
    ]

    barrier = pltpu.get_barrier_semaphore()
    each(lambda p, there: pl.semaphore_signal(
        barrier, inc=1, device_id=(there, core), device_id_type=MESH))
    pl.semaphore_signal(barrier, inc=1, device_id=(me, 1 - core), device_id_type=MESH)
    for load in loads:
        load.start()
    table = request_table(ids_ref[...], me, n, shard_rows)
    for p in range(n):
        req[p] = table[p : p + 1]
    want[n - 1] = table[n - 1 : n]
    pl.semaphore_wait(barrier, n)

    each(lambda p, there: ask(p, there).start())
    each(lambda p, there: ask(p, there).wait_recv())

    def columns(rows, into, change):
        rows_t = turned(rows)
        for p in range(n):
            into[p * CAP : (p + 1) * CAP, :] = jnp.broadcast_to(
                change(rows_t[:CAP, p : p + 1]), (CAP, LANES))

    wanted = want[:, 0, :]
    columns(wanted, wcol, lambda x: x)

    loads[0].wait()

    def gather(c):
        w = wcol[part(c), :]
        lane = iota((chunk, LANES), 1)
        hot = jnp.concatenate(
            [jnp.where(w == lane + k, 1.0, 0.0).astype(jnp.bfloat16)
             for k in range(0, shard_rows, LANES)], axis=1)
        send[part(c), :] = dot(hot, pas[...]).astype(jnp.bfloat16)

    def gather_and_send(c):
        gather(c)
        of_chunk(c, lambda p, there: fetch(p, there).start())

    ahead = min(4, chunks)
    loop(0, ahead, gather_and_send)

    block = min(256, queries)
    wide = min(512, queries)

    def block_at(b):
        return pl.ds(pl.multiple_of(b * block, block), block)

    def other_form():
        wrow[core] = slot_row(wanted, n)

    def mask():
        columns(req[:, 0, :], bias, lambda x: jnp.where(x >= 0, 0.0, NONE))

    def positive(b):
        both = q[block_at(b), :].astype(jnp.float32) * pos[block_at(b), :].astype(jnp.float32)
        total = both[:, :LANES]
        for k in range(LANES, depth, LANES):
            total = total + both[:, k : k + LANES]
        prow[:, block_at(b)] = scale * jnp.sum(total.T, axis=0, keepdims=True)

    def turn(b):
        wt[0:depth, block_at(b)] = q[block_at(b), :].T

    other_form()
    pass_row(core).start()
    mask()
    loads[1].wait()
    loads[2].wait()
    loop(0, queries // block, positive)
    loop(0, queries // block, turn)

    def logits(c):
        def one(b):
            at = pl.ds(pl.multiple_of(b * wide, wide), wide)
            x = scale * dot(got[part(c), :], wt[0:depth, at])
            x = x + jnp.concatenate([bias[part(c), :]] * (wide // LANES), axis=1)
            top = jnp.max(x, axis=0, keepdims=True)
            x = jnp.exp(x - top)
            big[part(c), at] = x
            tops[c, :, at] = top
            sums[c, :, at] = jnp.sum(x, axis=0, keepdims=True)

        loop(0, queries // wide, one)

    def receive(c):
        of_chunk(c, lambda p, there: fetch(p, there).wait_recv())

        @pl.when(c == chunks - 1)
        def _():
            got[slots - CAP : slots, :] = send[slots - CAP : slots, :]

        logits(c)

    def gather_or_receive(c):
        of_chunk(c - ahead, lambda p, there: fetch(p, there).wait_send())
        gather_and_send(c)
        receive(c - ahead)

    loop(ahead, chunks, gather_or_receive)
    loop(chunks - ahead, chunks, receive)

    def totals():
        pos_logit = prow[...]
        top = pos_logit
        for c in range(chunks):
            top = jnp.maximum(top, tops[c])
        pos_exp = jnp.exp(pos_logit - top)
        total = pos_exp
        for c in range(chunks):
            total = total + sums[c] * jnp.exp(tops[c] - top)
        for c in range(chunks):
            tops[c] = jnp.exp(tops[c] - top) * (factor / total)
        crow[...] = factor * (pos_exp / total - 1.0)
        loss_ref[...] = top + jnp.log(total) - pos_logit

    totals()

    loop(chunks - ahead, chunks,
         lambda c: of_chunk(c, lambda p, there: fetch(p, there).wait_send()))

    def row_grads(c):
        wt[part(c), :] = (big[part(c), :] * tops[c]).astype(jnp.bfloat16)
        send[part(c), :] = dot(wt[part(c), :], q[...]).astype(jnp.bfloat16)

    def return_rows(c):
        row_grads(c)
        of_chunk(c, lambda p, there: give(p, there).start())

    def out_q(b):
        return pltpu.make_async_copy(
            pas.at[block_at(b)], gq_hbm.at[block_at(b)], oq_s.at[b])

    def query_grads(b):
        g = dot(wt[:, block_at(b)], got[...], ((0,), (0,)))
        coef = jnp.broadcast_to(crow[:, block_at(b)], (LANES, block)).T
        coef = jnp.concatenate([coef] * (depth // LANES), axis=1)
        g = g + coef * pos[block_at(b), :].astype(jnp.float32)
        pas[block_at(b), :] = g.astype(jnp.bfloat16)

    def query_grads_out(b):
        query_grads(b)
        out_q(b).start()

    tall = min(512, shard_rows)

    def tall_at(b):
        return pl.ds(pl.multiple_of(b * tall, tall), tall)

    def clear(b):
        big[tall_at(b), 0:depth] = jnp.zeros((tall, depth), jnp.float32)

    loop(0, ahead, return_rows)

    def return_more(c):
        of_chunk(c - ahead, lambda p, there: give(p, there).wait_send())
        return_rows(c)

    loop(ahead, chunks, return_more)
    ret[home(n - 1, core), :] = send[slots - CAP : slots, :]
    loop(0, queries // block, query_grads_out)
    loop(0, shard_rows // tall, clear)
    pass_row(1 - core).wait_recv()

    def out_p(b):
        return pltpu.make_async_copy(
            got.at[tall_at(b)], gp_hbm.at[tall_at(b)], op_s.at[b])

    def added(c, b):
        here = iota((tall, chunk), 0) + b * tall
        hot = jnp.concatenate(
            [jnp.where(here == wrow[whose, :, part(c)], 1.0, 0.0).astype(jnp.bfloat16)
             for whose in range(2)], axis=1)
        return big[tall_at(b), 0:depth] + dot(hot, ret[pair(c), :])

    def add_up(c):
        def one(b):
            big[tall_at(b), 0:depth] = added(c, b)

        loop(0, shard_rows // tall, one)

    def add_last(b):
        got[tall_at(b), :] = added(chunks - 1, b).astype(jnp.bfloat16)

    def add_last_out(b):
        add_last(b)
        out_p(b).start()

    def take(c):
        of_chunk(c, lambda p, there: give(p, there).wait_recv())
        pass_on(c, core).start()

    def collect(c):
        take(c)
        pass_on(c - 1, 1 - core).wait_recv()
        add_up(c - 1)

    take(0)
    loop(1, chunks, collect)
    pass_on(chunks - 1, 1 - core).wait_recv()
    loop(0, shard_rows // tall, add_last_out)

    each(lambda p, there: ask(p, there).wait_send())
    loop(chunks - ahead, chunks,
         lambda c: of_chunk(c, lambda p, there: give(p, there).wait_send()))
    pass_row(core).wait_send()
    loop(0, chunks, lambda c: pass_on(c, core).wait_send())
    loop(0, queries // block, lambda b: out_q(b).wait())
    loop(0, shard_rows // tall, lambda b: out_p(b).wait())


def local(group, queries, positives, passages, negatives):
    n = lax.axis_size("idx")
    count, depth = queries.shape
    shard_rows = passages.shape[0]
    slots = n * CAP
    chunks = n // group
    block = min(256, count)
    tall = min(512, shard_rows)
    any_space = pl.BlockSpec(memory_space=pl.ANY)
    vmem = pl.BlockSpec(memory_space=pltpu.VMEM)
    dma = pltpu.SemaphoreType.DMA
    bf16, f32 = jnp.bfloat16, jnp.float32
    loss, grad_q, grad_p = pl.pallas_call(
        functools.partial(kernel, n, group),
        out_shape=(
            jax.ShapeDtypeStruct((1, count), f32),
            jax.ShapeDtypeStruct((count, depth), bf16),
            jax.ShapeDtypeStruct((shard_rows, depth), bf16),
        ),
        in_specs=[vmem, any_space, any_space, any_space],
        out_specs=(vmem, any_space, any_space),
        scratch_shapes=[
            pltpu.VMEM((count, depth), bf16),
            pltpu.VMEM((count, depth), bf16),
            pltpu.VMEM((shard_rows, depth), bf16),
            pltpu.VMEM((slots, depth), bf16),
            pltpu.VMEM((slots, depth), bf16),
            pltpu.VMEM((2 * slots, depth), bf16),
            pltpu.VMEM((slots, count), f32),
            pltpu.VMEM((slots, count), bf16),
            pltpu.VMEM((n, 1, LANES), jnp.int32),
            pltpu.VMEM((n, 1, LANES), jnp.int32),
            pltpu.VMEM((slots, LANES), jnp.int32),
            pltpu.VMEM((slots, LANES), f32),
            pltpu.VMEM((2, 1, slots), jnp.int32),
            pltpu.VMEM((chunks, 1, count), f32),
            pltpu.VMEM((chunks, 1, count), f32),
            pltpu.VMEM((1, count), f32),
            pltpu.VMEM((1, count), f32),
            dma((3,)),
            dma((n,)), dma((n,)),
            dma((n,)), dma((n,)),
            dma((n,)), dma((n,)),
            dma((chunks,)), dma((chunks,)),
            dma, dma,
            dma((count // block,)),
            dma((shard_rows // tall,)),
        ],
        compiler_params=pltpu.CompilerParams(
            collective_id=0, has_side_effects=True, vmem_limit_bytes=62 << 20
        ),
        cost_estimate=pl.CostEstimate(
            flops=12 * slots * count * depth, bytes_accessed=20 * count * depth,
            transcendentals=slots * count,
        ),
    )(negatives.reshape(1, -1), queries, positives, passages)
    return loss.reshape(-1), grad_q, grad_p


def solution(mesh, group=8):
    placed = (
        P(("idx", "enc"), None),
        P(("idx", "enc"), None),
        P("idx", None),
        P(("idx", "enc"), None),
    )
    return jax.shard_map(
        functools.partial(local, group),
        mesh=mesh,
        in_specs=placed,
        out_specs=(P(("idx", "enc")), P(("idx", "enc"), None), P("idx", None)),
        check_vma=False,
    )
```

```python
import functools
import math

import jax
import jax.numpy as jnp
from jax import lax
from jax.experimental import pallas as pl
from jax.experimental.pallas import tpu as pltpu
from jax.sharding import PartitionSpec as P

LSCALE = 32
CAP = 32
LANES = 128
MESH = pl.DeviceIdType.MESH
NONE = -1e30


def flip(u, v):
    if isinstance(u, int):
        return 1 - v if u else v
    return u + v - 2 * u * v


def place_bits(c, j, n, group):
    low = int(math.log2(group))
    count = int(math.log2(n))
    p = [1 - ((j >> k) & 1) for k in range(low)]
    p += [1 - lax.rem(lax.div(c, 1 << k), 2) for k in range(count - low)]
    if n != 64:
        return p
    t0, t1, b0, b1, a0, a1 = p
    return [t0, t1, flip(t0, a0), flip(t1, a1), flip(t0, b0), flip(t1, b1)]


def place_of(distance, n):
    if n != 64:
        return n - 1 - distance
    z, x, y = distance & 3, (distance >> 2) & 3, (distance >> 4) & 3
    return n - 1 - (((x ^ z) << 4) + ((y ^ z) << 2) + z)


def iota(shape, dim):
    return lax.broadcasted_iota(jnp.int32, shape, dim)


def dot(a, b, dims=((1,), (0,))):
    return lax.dot_general(a, b, (dims, ((), ())), preferred_element_type=jnp.float32)


def turned(rows):
    m = rows.shape[0]
    if m < LANES:
        rows = jnp.concatenate([rows, jnp.zeros((LANES - m, LANES), rows.dtype)], axis=0)
    return rows.T


def request_table(ids, me, n, shard_rows):
    slots = ids.shape[1]
    shift = int(math.log2(shard_rows))
    live = ids >= 0
    place = place_of(jnp.bitwise_xor(lax.shift_right_arithmetic(ids, shift), me), n)
    place = jnp.where(live, place, -1)
    row = jnp.bitwise_and(ids, shard_rows - 1) + 1
    hot = iota((n, slots), 0) == place
    hot_f = jnp.where(hot, 1.0, 0.0)
    width = min(256, slots)
    before = jnp.where(
        iota((width, width), 0) < iota((width, width), 1), 1.0, 0.0
    ).astype(jnp.bfloat16)
    carry = jnp.zeros((n, 1), jnp.float32)
    ranks = []
    for at in range(0, slots, width):
        part = hot_f[:, at : at + width]
        ahead = dot(part.astype(jnp.bfloat16), before) + carry
        ranks.append(jnp.sum(part * ahead, axis=0, keepdims=True))
        carry = carry + jnp.sum(part, axis=1, keepdims=True)
    rank = jnp.concatenate(ranks, axis=1).astype(jnp.int32)
    of_rank = jnp.where(iota((LANES, slots), 0) == rank, 1.0, 0.0).astype(jnp.bfloat16)
    high = lax.shift_right_arithmetic(row, 6).astype(jnp.float32)
    low = jnp.bitwise_and(row, 63).astype(jnp.float32)
    values = jnp.concatenate([hot_f * high, hot_f * low], axis=0).astype(jnp.bfloat16)
    table = dot(values, of_rank, ((1,), (1,)))
    return (table[:n] * 64.0 + table[n:]).astype(jnp.int32) - 1


def slot_row(table, n):
    slots = n * CAP
    shifted = table + 1
    high = lax.shift_right_arithmetic(shifted, 6).astype(jnp.float32)
    low = jnp.bitwise_and(shifted, 63).astype(jnp.float32)
    parts = jnp.concatenate([high, low], axis=0).astype(jnp.bfloat16)
    lane = jnp.bitwise_and(iota((LANES, slots), 1), CAP - 1)
    spread = jnp.where(iota((LANES, slots), 0) == lane, 1.0, 0.0).astype(jnp.bfloat16)
    wide = dot(parts, spread)
    both = wide[:n] * 64.0 + wide[n:]
    mine = lax.shift_right_arithmetic(iota((n, slots), 1), 5) == iota((n, slots), 0)
    row = jnp.sum(jnp.where(mine, both, 0.0), axis=0, keepdims=True)
    return row.astype(jnp.int32) - 1


def kernel(
    n, group,
    ids_ref, q_hbm, pos_hbm, pas_hbm,
    loss_ref, pas, pos,
    q, send, got, ret, big, wt,
    req, want, wcol, bias, wrow, tops, sums, prow, crow,
    load_s, rq_s, rq_r, f_s, f_r, r_s, r_r, fw_s, fw_r, wx_s, wx_r,
):
    me, core = lax.axis_index("idx"), lax.axis_index("enc")
    queries, depth = q.shape
    shard_rows = pas.shape[0]
    slots = n * CAP
    chunk = group * CAP
    chunks = n // group
    scale = 3.0 / math.sqrt(depth)
    factor = LSCALE * scale
    steps = [
        (1 << k) * (1 - 2 * lax.rem(lax.div(me, 1 << k), 2))
        for k in range(int(math.log2(n)))
    ]

    def partner(c, j):
        bits = place_bits(c, j, n, group)
        there = me
        for bit, step in zip(bits, steps):
            if isinstance(bit, int):
                there = there + step if bit else there
            else:
                there = there + bit * step
        return there

    def of_chunk(c, work):
        for j in range(group):
            if j == group - 1:
                @pl.when(c < chunks - 1)
                def _():
                    work(c * group + j, partner(c, j))
            else:
                work(c * group + j, partner(c, j))

    def loop(start, stop, body):
        def step(c, carry):
            body(c)
            return carry

        lax.fori_loop(start, stop, step, 0)

    def each(work):
        loop(0, chunks, lambda c: of_chunk(c, work))

    def part(c):
        return pl.ds(pl.multiple_of(c * chunk, chunk), chunk)

    def rows_at(p):
        return pl.ds(pl.multiple_of(p * CAP, CAP), CAP)

    def pair(c):
        return pl.ds(pl.multiple_of(c * 2 * chunk, 2 * chunk), 2 * chunk)

    def half(c, whose):
        return pl.ds(pl.multiple_of((c * 2 + whose) * chunk, chunk), chunk)

    def home(p, whose):
        c, j = lax.div(p, group), lax.rem(p, group)
        return pl.ds(pl.multiple_of((c * 2 + whose) * chunk + j * CAP, CAP), CAP)

    def ask(p, there):
        return pltpu.make_async_remote_copy(
            src_ref=req.at[p], dst_ref=want.at[p], send_sem=rq_s.at[p],
            recv_sem=rq_r.at[p], device_id=(there, core), device_id_type=MESH)

    def fetch(p, there):
        return pltpu.make_async_remote_copy(
            src_ref=send.at[rows_at(p)], dst_ref=got.at[rows_at(p)], send_sem=f_s.at[p],
            recv_sem=f_r.at[p], device_id=(there, core), device_id_type=MESH)

    def give(p, there):
        return pltpu.make_async_remote_copy(
            src_ref=send.at[rows_at(p)], dst_ref=ret.at[home(p, core)], send_sem=r_s.at[p],
            recv_sem=r_r.at[p], device_id=(there, core), device_id_type=MESH)

    def pass_on(c, whose):
        return pltpu.make_async_remote_copy(
            src_ref=ret.at[half(c, whose)], dst_ref=ret.at[half(c, whose)],
            send_sem=fw_s.at[c], recv_sem=fw_r.at[c],
            device_id=(me, 1 - core), device_id_type=MESH)

    def pass_row(whose):
        return pltpu.make_async_remote_copy(
            src_ref=wrow.at[whose], dst_ref=wrow.at[whose], send_sem=wx_s, recv_sem=wx_r,
            device_id=(me, 1 - core), device_id_type=MESH)

    loads = [
        pltpu.make_async_copy(src, dst, load_s.at[k])
        for k, (src, dst) in enumerate([(pas_hbm, pas), (q_hbm, q), (pos_hbm, pos)])
    ]

    barrier = pltpu.get_barrier_semaphore()
    each(lambda p, there: pl.semaphore_signal(
        barrier, inc=1, device_id=(there, core), device_id_type=MESH))
    pl.semaphore_signal(barrier, inc=1, device_id=(me, 1 - core), device_id_type=MESH)
    for load in loads:
        load.start()
    table = request_table(ids_ref[...], me, n, shard_rows)
    for p in range(n):
        req[p] = table[p : p + 1]
    want[n - 1] = table[n - 1 : n]
    pl.semaphore_wait(barrier, n)

    each(lambda p, there: ask(p, there).start())
    each(lambda p, there: ask(p, there).wait_recv())

    def columns(rows, into, change):
        rows_t = turned(rows)
        for p in range(n):
            into[p * CAP : (p + 1) * CAP, :] = jnp.broadcast_to(
                change(rows_t[:CAP, p : p + 1]), (CAP, LANES))

    wanted = want[:, 0, :]
    columns(wanted, wcol, lambda x: x)

    loads[0].wait()

    def gather(c):
        w = wcol[part(c), :]
        lane = iota((chunk, LANES), 1)
        hot = jnp.concatenate(
            [jnp.where(w == lane + k, 1.0, 0.0).astype(jnp.bfloat16)
             for k in range(0, shard_rows, LANES)], axis=1)
        send[part(c), :] = dot(hot, pas[...]).astype(jnp.bfloat16)

    def gather_and_send(c):
        gather(c)
        of_chunk(c, lambda p, there: fetch(p, there).start())

    ahead = chunks
    loop(0, ahead, gather_and_send)

    block = min(256, queries)
    wide = min(512, queries)

    def block_at(b):
        return pl.ds(pl.multiple_of(b * block, block), block)

    def other_form():
        wrow[core] = slot_row(wanted, n)

    def mask():
        columns(req[:, 0, :], bias, lambda x: jnp.where(x >= 0, 0.0, NONE))

    def positive(b):
        both = q[block_at(b), :].astype(jnp.float32) * pos[block_at(b), :].astype(jnp.float32)
        total = both[:, :LANES]
        for k in range(LANES, depth, LANES):
            total = total + both[:, k : k + LANES]
        prow[:, block_at(b)] = scale * jnp.sum(total.T, axis=0, keepdims=True)

    def turn(b):
        wt[0:depth, block_at(b)] = q[block_at(b), :].T

    other_form()
    pass_row(core).start()
    mask()
    loads[1].wait()
    loads[2].wait()
    loop(0, queries // block, positive)
    loop(0, queries // block, turn)

    def logits(c):
        def one(b):
            at = pl.ds(pl.multiple_of(b * wide, wide), wide)
            x = scale * dot(got[part(c), :], wt[0:depth, at])
            x = x + jnp.concatenate([bias[part(c), :]] * (wide // LANES), axis=1)
            top = jnp.max(x, axis=0, keepdims=True)
            x = jnp.exp(x - top)
            big[part(c), at] = x
            tops[c, :, at] = top
            sums[c, :, at] = jnp.sum(x, axis=0, keepdims=True)

        loop(0, queries // wide, one)

    def receive(c):
        of_chunk(c, lambda p, there: fetch(p, there).wait_recv())

        @pl.when(c == chunks - 1)
        def _():
            got[slots - CAP : slots, :] = send[slots - CAP : slots, :]

        logits(c)

    def gather_or_receive(c):
        of_chunk(c - ahead, lambda p, there: fetch(p, there).wait_send())
        gather_and_send(c)
        receive(c - ahead)

    loop(ahead, chunks, gather_or_receive)
    loop(chunks - ahead, chunks, receive)

    def totals():
        pos_logit = prow[...]
        top = pos_logit
        for c in range(chunks):
            top = jnp.maximum(top, tops[c])
        pos_exp = jnp.exp(pos_logit - top)
        total = pos_exp
        for c in range(chunks):
            total = total + sums[c] * jnp.exp(tops[c] - top)
        for c in range(chunks):
            tops[c] = jnp.exp(tops[c] - top) * (factor / total)
        crow[...] = factor * (pos_exp / total - 1.0)
        loss_ref[...] = top + jnp.log(total) - pos_logit

    totals()

    loop(chunks - ahead, chunks,
         lambda c: of_chunk(c, lambda p, there: fetch(p, there).wait_send()))

    def row_grads(c):
        wt[part(c), :] = (big[part(c), :] * tops[c]).astype(jnp.bfloat16)
        send[part(c), :] = dot(wt[part(c), :], q[...]).astype(jnp.bfloat16)

    def return_rows(c):
        row_grads(c)
        of_chunk(c, lambda p, there: give(p, there).start())

    def query_grads(b):
        g = dot(wt[:, block_at(b)], got[...], ((0,), (0,)))
        coef = jnp.broadcast_to(crow[:, block_at(b)], (LANES, block)).T
        coef = jnp.concatenate([coef] * (depth // LANES), axis=1)
        g = g + coef * pos[block_at(b), :].astype(jnp.float32)
        pas[block_at(b), :] = g.astype(jnp.bfloat16)

    tall = min(512, shard_rows)

    def tall_at(b):
        return pl.ds(pl.multiple_of(b * tall, tall), tall)

    def clear(b):
        big[tall_at(b), 0:depth] = jnp.zeros((tall, depth), jnp.float32)

    loop(0, ahead, return_rows)

    def return_more(c):
        of_chunk(c - ahead, lambda p, there: give(p, there).wait_send())
        return_rows(c)

    loop(ahead, chunks, return_more)
    ret[home(n - 1, core), :] = send[slots - CAP : slots, :]
    loop(0, queries // block, query_grads)
    loop(0, shard_rows // tall, clear)
    pass_row(1 - core).wait_recv()

    def added(c, b):
        here = iota((tall, chunk), 0) + b * tall
        hot = jnp.concatenate(
            [jnp.where(here == wrow[whose, :, part(c)], 1.0, 0.0).astype(jnp.bfloat16)
             for whose in range(2)], axis=1)
        return big[tall_at(b), 0:depth] + dot(hot, ret[pair(c), :])

    def add_up(c):
        def one(b):
            big[tall_at(b), 0:depth] = added(c, b)

        loop(0, shard_rows // tall, one)

    def add_last(b):
        pos[tall_at(b), :] = added(chunks - 1, b).astype(jnp.bfloat16)

    def take(c):
        of_chunk(c, lambda p, there: give(p, there).wait_recv())
        pass_on(c, core).start()

    def collect(c):
        take(c)
        pass_on(c - 1, 1 - core).wait_recv()
        add_up(c - 1)

    take(0)
    loop(1, chunks, collect)
    pass_on(chunks - 1, 1 - core).wait_recv()
    loop(0, shard_rows // tall, add_last)

    each(lambda p, there: ask(p, there).wait_send())
    loop(chunks - ahead, chunks,
         lambda c: of_chunk(c, lambda p, there: give(p, there).wait_send()))
    pass_row(core).wait_send()
    loop(0, chunks, lambda c: pass_on(c, core).wait_send())


def local(group, queries, positives, passages, negatives):
    n = lax.axis_size("idx")
    count, depth = queries.shape
    shard_rows = passages.shape[0]
    slots = n * CAP
    chunks = n // group
    any_space = pl.BlockSpec(memory_space=pl.ANY)
    vmem = pl.BlockSpec(memory_space=pltpu.VMEM)
    dma = pltpu.SemaphoreType.DMA
    bf16, f32 = jnp.bfloat16, jnp.float32
    loss, grad_q, grad_p = pl.pallas_call(
        functools.partial(kernel, n, group),
        out_shape=(
            jax.ShapeDtypeStruct((1, count), f32),
            pltpu.VMEM((count, depth), bf16),
            pltpu.VMEM((shard_rows, depth), bf16),
        ),
        in_specs=[vmem, any_space, any_space, any_space],
        out_specs=(vmem, vmem, vmem),
        scratch_shapes=[
            pltpu.VMEM((count, depth), bf16),
            pltpu.VMEM((slots, depth), bf16),
            pltpu.VMEM((slots, depth), bf16),
            pltpu.VMEM((2 * slots, depth), bf16),
            pltpu.VMEM((slots, count), f32),
            pltpu.VMEM((slots, count), bf16),
            pltpu.VMEM((n, 1, LANES), jnp.int32),
            pltpu.VMEM((n, 1, LANES), jnp.int32),
            pltpu.VMEM((slots, LANES), jnp.int32),
            pltpu.VMEM((slots, LANES), f32),
            pltpu.VMEM((2, 1, slots), jnp.int32),
            pltpu.VMEM((chunks, 1, count), f32),
            pltpu.VMEM((chunks, 1, count), f32),
            pltpu.VMEM((1, count), f32),
            pltpu.VMEM((1, count), f32),
            dma((3,)),
            dma((n,)), dma((n,)),
            dma((n,)), dma((n,)),
            dma((n,)), dma((n,)),
            dma((chunks,)), dma((chunks,)),
            dma, dma,
        ],
        compiler_params=pltpu.CompilerParams(
            collective_id=0, has_side_effects=True, vmem_limit_bytes=52 << 20
        ),
        cost_estimate=pl.CostEstimate(
            flops=12 * slots * count * depth, bytes_accessed=20 * count * depth,
            transcendentals=slots * count,
        ),
    )(negatives.reshape(1, -1), queries, positives, passages)
    return loss.reshape(-1), grad_q, grad_p


def solution(mesh, group=8):
    placed = (
        P(("idx", "enc"), None),
        P(("idx", "enc"), None),
        P("idx", None),
        P(("idx", "enc"), None),
    )
    return jax.shard_map(
        functools.partial(local, group),
        mesh=mesh,
        in_specs=placed,
        out_specs=(P(("idx", "enc")), P(("idx", "enc"), None), P("idx", None)),
        check_vma=False,
    )
```

```python
import functools
import math

import jax
import jax.numpy as jnp
from jax import lax
from jax.experimental import pallas as pl
from jax.experimental.pallas import tpu as pltpu
from jax.sharding import PartitionSpec as P

LSCALE = 32
CAP = 32
LANES = 128
MESH = pl.DeviceIdType.MESH
NONE = -1e30


def flip(u, v):
    if isinstance(u, int):
        return 1 - v if u else v
    return u + v - 2 * u * v


def place_bits(c, j, n, group):
    low = int(math.log2(group))
    count = int(math.log2(n))
    p = [(j >> k) & 1 for k in range(low)]
    p += [lax.rem(lax.div(c, 1 << k), 2) for k in range(count - low)]
    if n != 64:
        return p
    t0, t1, b0, b1, a0, a1 = p
    return [t0, t1, flip(t0, a0), flip(t1, a1), flip(t0, b0), flip(t1, b1)]


def place_of(distance, n):
    if n != 64:
        return distance
    z, x, y = distance & 3, (distance >> 2) & 3, (distance >> 4) & 3
    return ((x ^ z) << 4) + ((y ^ z) << 2) + z


def iota(shape, dim):
    return lax.broadcasted_iota(jnp.int32, shape, dim)


def dot(a, b, dims=((1,), (0,))):
    return lax.dot_general(a, b, (dims, ((), ())), preferred_element_type=jnp.float32)


def turned(rows):
    m = rows.shape[0]
    if m < LANES:
        rows = jnp.concatenate([rows, jnp.zeros((LANES - m, LANES), rows.dtype)], axis=0)
    return rows.T


def request_table(ids, me, n, shard_rows):
    slots = ids.shape[1]
    shift = int(math.log2(shard_rows))
    live = ids >= 0
    place = place_of(jnp.bitwise_xor(lax.shift_right_arithmetic(ids, shift), me), n)
    place = jnp.where(live, place, -1)
    row = jnp.bitwise_and(ids, shard_rows - 1) + 1
    hot = iota((n, slots), 0) == place
    hot_f = jnp.where(hot, 1.0, 0.0)
    width = min(256, slots)
    before = jnp.where(
        iota((width, width), 0) < iota((width, width), 1), 1.0, 0.0
    ).astype(jnp.bfloat16)
    carry = jnp.zeros((n, 1), jnp.float32)
    ranks = []
    for at in range(0, slots, width):
        part = hot_f[:, at : at + width]
        ahead = dot(part.astype(jnp.bfloat16), before) + carry
        ranks.append(jnp.sum(part * ahead, axis=0, keepdims=True))
        carry = carry + jnp.sum(part, axis=1, keepdims=True)
    rank = jnp.concatenate(ranks, axis=1).astype(jnp.int32)
    of_rank = jnp.where(iota((LANES, slots), 0) == rank, 1.0, 0.0).astype(jnp.bfloat16)
    high = lax.shift_right_arithmetic(row, 6).astype(jnp.float32)
    low = jnp.bitwise_and(row, 63).astype(jnp.float32)
    values = jnp.concatenate([hot_f * high, hot_f * low], axis=0).astype(jnp.bfloat16)
    table = dot(values, of_rank, ((1,), (1,)))
    return (table[:n] * 64.0 + table[n:]).astype(jnp.int32) - 1


def slot_row(table, n):
    slots = n * CAP
    shifted = table + 1
    high = lax.shift_right_arithmetic(shifted, 6).astype(jnp.float32)
    low = jnp.bitwise_and(shifted, 63).astype(jnp.float32)
    parts = jnp.concatenate([high, low], axis=0).astype(jnp.bfloat16)
    lane = jnp.bitwise_and(iota((LANES, slots), 1), CAP - 1)
    spread = jnp.where(iota((LANES, slots), 0) == lane, 1.0, 0.0).astype(jnp.bfloat16)
    wide = dot(parts, spread)
    both = wide[:n] * 64.0 + wide[n:]
    mine = lax.shift_right_arithmetic(iota((n, slots), 1), 5) == iota((n, slots), 0)
    row = jnp.sum(jnp.where(mine, both, 0.0), axis=0, keepdims=True)
    return row.astype(jnp.int32) - 1


def kernel(
    n, group,
    ids_ref, q_hbm, pos_hbm, pas_hbm,
    loss_ref, pas, pos,
    q, send, got, ret, big, wt,
    req, want, wcol, bias, wrow, tops, sums, prow, crow,
    load_s, rq_s, rq_r, f_s, f_r, r_s, r_r, wx_s, wx_r, sw_s, sw_r, free_s,
):
    me, core = lax.axis_index("idx"), lax.axis_index("enc")
    queries, depth = q.shape
    shard_rows = pas.shape[0]
    slots = n * CAP
    chunk = group * CAP
    chunks = n // group
    scale = 3.0 / math.sqrt(depth)
    factor = LSCALE * scale
    cut = depth // 2
    steps = [
        (1 << k) * (1 - 2 * lax.rem(lax.div(me, 1 << k), 2))
        for k in range(int(math.log2(n)))
    ]

    def partner(c, j):
        bits = place_bits(c, j, n, group)
        there = me
        for bit, step in zip(bits, steps):
            if isinstance(bit, int):
                there = there + step if bit else there
            else:
                there = there + bit * step
        return there

    def of_chunk(c, work):
        for j in range(group):
            if j == 0:
                @pl.when(c > 0)
                def _():
                    work(c * group + j, partner(c, j))
            else:
                work(c * group + j, partner(c, j))

    def loop(start, stop, body):
        def step(c, carry):
            body(c)
            return carry

        lax.fori_loop(start, stop, step, 0)

    def each(work):
        loop(0, chunks, lambda c: of_chunk(c, work))

    def part(c):
        return pl.ds(pl.multiple_of(c * chunk, chunk), chunk)

    def rows_at(p):
        return pl.ds(pl.multiple_of(p * CAP, CAP), CAP)

    def pair(c):
        return pl.ds(pl.multiple_of(c * 2 * chunk, 2 * chunk), 2 * chunk)

    def home(p, whose):
        c, j = lax.div(p, group), lax.rem(p, group)
        return pl.ds(pl.multiple_of((c * 2 + whose) * chunk + j * CAP, CAP), CAP)

    def ask(p, there):
        return pltpu.make_async_remote_copy(
            src_ref=req.at[p], dst_ref=want.at[p], send_sem=rq_s.at[p],
            recv_sem=rq_r.at[p], device_id=(there, core), device_id_type=MESH)

    def fetch(p, there):
        return pltpu.make_async_remote_copy(
            src_ref=send.at[rows_at(p)], dst_ref=got.at[rows_at(p)], send_sem=f_s.at[p],
            recv_sem=f_r.at[p], device_id=(there, core), device_id_type=MESH)

    def give(p, there, side):
        return pltpu.make_async_remote_copy(
            src_ref=send.at[rows_at(p), pl.ds(pl.multiple_of(side * cut, cut), cut)],
            dst_ref=ret.at[home(p, core)], send_sem=r_s.at[side, p],
            recv_sem=r_r.at[core, p], device_id=(there, side), device_id_type=MESH)

    def given(p, whose):
        return pltpu.make_async_remote_copy(
            src_ref=ret.at[home(p, whose)], dst_ref=ret.at[home(p, whose)],
            send_sem=r_s.at[whose, p], recv_sem=r_r.at[whose, p],
            device_id=(me, 1 - core), device_id_type=MESH)

    def pass_row(whose):
        return pltpu.make_async_remote_copy(
            src_ref=wrow.at[whose], dst_ref=wrow.at[whose], send_sem=wx_s, recv_sem=wx_r,
            device_id=(me, 1 - core), device_id_type=MESH)

    loads = [
        pltpu.make_async_copy(src, dst, load_s.at[k])
        for k, (src, dst) in enumerate([(pas_hbm, pas), (q_hbm, q), (pos_hbm, pos)])
    ]

    barrier = pltpu.get_barrier_semaphore()
    each(lambda p, there: pl.semaphore_signal(
        barrier, inc=1, device_id=(there, core), device_id_type=MESH))
    pl.semaphore_signal(barrier, inc=1, device_id=(me, 1 - core), device_id_type=MESH)
    for load in loads:
        load.start()
    table = request_table(ids_ref[...], me, n, shard_rows)
    for p in range(n):
        req[p] = table[p : p + 1]
    want[0] = table[0:1]
    pl.semaphore_wait(barrier, n)

    each(lambda p, there: ask(p, there).start())
    each(lambda p, there: ask(p, there).wait_recv())

    def columns(rows, into, change):
        rows_t = turned(rows)
        for p in range(n):
            into[p * CAP : (p + 1) * CAP, :] = jnp.broadcast_to(
                change(rows_t[:CAP, p : p + 1]), (CAP, LANES))

    wanted = want[:, 0, :]
    columns(wanted, wcol, lambda x: x)

    loads[0].wait()

    def gather(c):
        w = wcol[part(c), :]
        lane = iota((chunk, LANES), 1)
        hot = jnp.concatenate(
            [jnp.where(w == lane + k, 1.0, 0.0).astype(jnp.bfloat16)
             for k in range(0, shard_rows, LANES)], axis=1)
        send[part(c), :] = dot(hot, pas[...]).astype(jnp.bfloat16)

    def gather_and_send(c):
        gather(c)
        of_chunk(c, lambda p, there: fetch(p, there).start())

    loop(0, chunks, gather_and_send)
    got[0:CAP, :] = send[0:CAP, :]

    block = min(256, queries)
    wide = min(512, queries)

    def block_at(b):
        return pl.ds(pl.multiple_of(b * block, block), block)

    def other_form():
        wrow[core] = slot_row(wanted, n)

    def mask():
        columns(req[:, 0, :], bias, lambda x: jnp.where(x >= 0, 0.0, NONE))

    def positive(b):
        both = q[block_at(b), :].astype(jnp.float32) * pos[block_at(b), :].astype(jnp.float32)
        total = both[:, :LANES]
        for k in range(LANES, depth, LANES):
            total = total + both[:, k : k + LANES]
        prow[:, block_at(b)] = scale * jnp.sum(total.T, axis=0, keepdims=True)

    def turn(b):
        wt[0:depth, block_at(b)] = q[block_at(b), :].T

    other_form()
    pass_row(core).start()
    mask()
    loads[1].wait()
    loads[2].wait()
    loop(0, queries // block, positive)
    loop(0, queries // block, turn)

    power = scale * math.log2(math.e)

    def logits(c):
        def product(at):
            return dot(got[part(c), :], wt[0:depth, at : at + wide])

        ahead = product(0)
        for at in range(0, queries, wide):
            x = ahead
            if at + wide < queries:
                ahead = product(at + wide)
            x = x + jnp.concatenate([bias[part(c), :]] * (wide // LANES), axis=1)
            top = jnp.max(x, axis=0, keepdims=True)
            x = jnp.exp2(power * (x - top))
            big[part(c), at : at + wide] = x
            tops[c, :, at : at + wide] = scale * top
            sums[c, :, at : at + wide] = jnp.sum(x, axis=0, keepdims=True)

    def receive(c):
        of_chunk(c, lambda p, there: fetch(p, there).wait_recv())

        logits(c)

    loop(0, chunks, receive)

    def totals():
        pos_logit = prow[...]
        top = pos_logit
        for c in range(chunks):
            top = jnp.maximum(top, tops[c])
        pos_exp = jnp.exp(pos_logit - top)
        total = pos_exp
        for c in range(chunks):
            total = total + sums[c] * jnp.exp(tops[c] - top)
        for c in range(chunks):
            tops[c] = jnp.exp(tops[c] - top) * (factor / total)
        crow[...] = factor * (pos_exp / total - 1.0)
        loss_ref[...] = top + jnp.log(total) - pos_logit

    totals()

    each(lambda p, there: fetch(p, there).wait_send())

    def row_grads(c):
        wt[part(c), :] = (big[part(c), :] * tops[c]).astype(jnp.bfloat16)
        send[part(c), :] = dot(wt[part(c), :], q[...]).astype(jnp.bfloat16)

    def return_rows(c):
        row_grads(c)

        @pl.when(c == 0)
        def _():
            give(0, me, 1 - core).start()

        def both(p, there):
            give(p, there, 0).start()
            give(p, there, 1).start()

        of_chunk(c, both)

    def wide_at(b):
        return pl.ds(pl.multiple_of(b * wide, wide), wide)

    def query_grads(b):
        g = dot(wt[:, wide_at(b)], got[...], ((0,), (0,)))
        coef = jnp.broadcast_to(crow[:, wide_at(b)], (LANES, wide)).T
        coef = jnp.concatenate([coef] * (depth // LANES), axis=1)
        g = g + coef * pos[wide_at(b), :].astype(jnp.float32)
        pas[wide_at(b), :] = g.astype(jnp.bfloat16)

    tall = min(512, shard_rows)

    def tall_at(b):
        return pl.ds(pl.multiple_of(b * tall, tall), tall)

    def clear(b):
        big[tall_at(b), 0:cut] = jnp.zeros((tall, cut), jnp.float32)

    loop(0, chunks, return_rows)
    mine = pl.ds(pl.multiple_of(core * cut, cut), cut)
    ret[home(0, core), :] = send[0:CAP, mine]
    loop(0, queries // wide, query_grads)
    pl.semaphore_signal(free_s, inc=1, device_id=(me, 1 - core), device_id_type=MESH)
    loop(0, shard_rows // tall, clear)
    pass_row(1 - core).wait_recv()

    def added(c, b):
        here = iota((tall, chunk), 0) + b * tall
        hot = jnp.concatenate(
            [jnp.where(here == wrow[whose, :, part(c)], 1.0, 0.0).astype(jnp.bfloat16)
             for whose in range(2)], axis=1)
        return big[tall_at(b), 0:cut] + dot(hot, ret[pair(c), :])

    def add_up(c):
        for b in range(shard_rows // tall):
            big[tall_at(b), 0:cut] = added(c, b)

    def add_last(b):
        pos[tall_at(b), mine] = added(chunks - 1, b).astype(jnp.bfloat16)

    def swap(b, side):
        block = pos.at[tall_at(b), pl.ds(pl.multiple_of(side * cut, cut), cut)]
        return pltpu.make_async_remote_copy(
            src_ref=block, dst_ref=block, send_sem=sw_s.at[b], recv_sem=sw_r.at[b],
            device_id=(me, 1 - core), device_id_type=MESH)

    def take(c):
        def both(p, there):
            given(p, 0).wait_recv()
            given(p, 1).wait_recv()

        of_chunk(c, both)

    def collect(c):
        take(c)
        add_up(c)

    given(0, 1 - core).wait_recv()
    loop(0, chunks - 1, collect)
    take(chunks - 1)
    pl.semaphore_wait(free_s, 1)
    for b in range(shard_rows // tall):
        add_last(b)
        swap(b, core).start()

    each(lambda p, there: ask(p, there).wait_send())

    def sent(p, there):
        give(p, there, 0).wait_send()
        give(p, there, 1).wait_send()

    each(sent)
    give(0, me, 1 - core).wait_send()
    pass_row(core).wait_send()
    for b in range(shard_rows // tall):
        swap(b, core).wait_send()
        swap(b, 1 - core).wait_recv()


def local(group, queries, positives, passages, negatives):
    n = lax.axis_size("idx")
    count, depth = queries.shape
    shard_rows = passages.shape[0]
    slots = n * CAP
    chunks = n // group
    any_space = pl.BlockSpec(memory_space=pl.ANY)
    vmem = pl.BlockSpec(memory_space=pltpu.VMEM)
    dma = pltpu.SemaphoreType.DMA
    bf16, f32 = jnp.bfloat16, jnp.float32
    loss, grad_q, grad_p = pl.pallas_call(
        functools.partial(kernel, n, group),
        out_shape=(
            jax.ShapeDtypeStruct((1, count), f32),
            pltpu.VMEM((count, depth), bf16),
            pltpu.VMEM((shard_rows, depth), bf16),
        ),
        in_specs=[vmem, any_space, any_space, any_space],
        out_specs=(vmem, vmem, vmem),
        scratch_shapes=[
            pltpu.VMEM((count, depth), bf16),
            pltpu.VMEM((slots, depth), bf16),
            pltpu.VMEM((slots, depth), bf16),
            pltpu.VMEM((2 * slots, depth // 2), bf16),
            pltpu.VMEM((slots, count), f32),
            pltpu.VMEM((slots, count), bf16),
            pltpu.VMEM((n, 1, LANES), jnp.int32),
            pltpu.VMEM((n, 1, LANES), jnp.int32),
            pltpu.VMEM((slots, LANES), jnp.int32),
            pltpu.VMEM((slots, LANES), f32),
            pltpu.VMEM((2, 1, slots), jnp.int32),
            pltpu.VMEM((chunks, 1, count), f32),
            pltpu.VMEM((chunks, 1, count), f32),
            pltpu.VMEM((1, count), f32),
            pltpu.VMEM((1, count), f32),
            dma((3,)),
            dma((n,)), dma((n,)),
            dma((n,)), dma((n,)),
            dma((2, n)), dma((2, n)),
            dma, dma,
            dma((shard_rows // min(512, shard_rows),)),
            dma((shard_rows // min(512, shard_rows),)),
            pltpu.SemaphoreType.REGULAR,
        ],
        compiler_params=pltpu.CompilerParams(
            collective_id=0, has_side_effects=True, vmem_limit_bytes=52 << 20
        ),
        cost_estimate=pl.CostEstimate(
            flops=12 * slots * count * depth, bytes_accessed=20 * count * depth,
            transcendentals=slots * count,
        ),
    )(negatives.reshape(1, -1), queries, positives, passages)
    return loss.reshape(-1), grad_q, grad_p


def solution(mesh, group=8):
    placed = (
        P(("idx", "enc"), None),
        P(("idx", "enc"), None),
        P("idx", None),
        P(("idx", "enc"), None),
    )
    return jax.shard_map(
        functools.partial(local, group),
        mesh=mesh,
        in_specs=placed,
        out_specs=(P(("idx", "enc")), P(("idx", "enc"), None), P("idx", None)),
        check_vma=False,
    )
```

```python
import functools
import math

import jax
import jax.numpy as jnp
from jax import lax
from jax.experimental import pallas as pl
from jax.experimental.pallas import tpu as pltpu
from jax.sharding import PartitionSpec as P

LSCALE = 32
CAP = 32
LANES = 128
MESH = pl.DeviceIdType.MESH
NONE = -1e30


def flip(u, v):
    if isinstance(u, int):
        return 1 - v if u else v
    return u + v - 2 * u * v


def place_bits(c, j, n, group):
    low = int(math.log2(group))
    count = int(math.log2(n))
    p = [(j >> k) & 1 for k in range(low)]
    p += [lax.rem(lax.div(c, 1 << k), 2) for k in range(count - low)]
    if n != 64:
        return p
    t0, t1, b0, b1, a0, a1 = p
    return [t0, t1, flip(t0, a0), flip(t1, a1), flip(t0, b0), flip(t1, b1)]


def place_of(distance, n):
    if n != 64:
        return distance
    z, x, y = distance & 3, (distance >> 2) & 3, (distance >> 4) & 3
    return ((x ^ z) << 4) + ((y ^ z) << 2) + z


def iota(shape, dim):
    return lax.broadcasted_iota(jnp.int32, shape, dim)


def dot(a, b, dims=((1,), (0,))):
    return lax.dot_general(a, b, (dims, ((), ())), preferred_element_type=jnp.float32)


def turned(rows):
    m = rows.shape[0]
    if m < LANES:
        rows = jnp.concatenate([rows, jnp.zeros((LANES - m, LANES), rows.dtype)], axis=0)
    return rows.T


def request_table(ids, me, n, shard_rows):
    slots = ids.shape[1]
    shift = int(math.log2(shard_rows))
    live = ids >= 0
    place = place_of(jnp.bitwise_xor(lax.shift_right_arithmetic(ids, shift), me), n)
    place = jnp.where(live, place, -1)
    row = jnp.bitwise_and(ids, shard_rows - 1) + 1
    hot = iota((n, slots), 0) == place
    hot_f = jnp.where(hot, 1.0, 0.0)
    width = min(256, slots)
    before = jnp.where(
        iota((width, width), 0) < iota((width, width), 1), 1.0, 0.0
    ).astype(jnp.bfloat16)
    carry = jnp.zeros((n, 1), jnp.float32)
    ranks = []
    for at in range(0, slots, width):
        part = hot_f[:, at : at + width]
        ahead = dot(part.astype(jnp.bfloat16), before) + carry
        ranks.append(jnp.sum(part * ahead, axis=0, keepdims=True))
        carry = carry + jnp.sum(part, axis=1, keepdims=True)
    rank = jnp.concatenate(ranks, axis=1).astype(jnp.int32)
    of_rank = jnp.where(iota((LANES, slots), 0) == rank, 1.0, 0.0).astype(jnp.bfloat16)
    high = lax.shift_right_arithmetic(row, 6).astype(jnp.float32)
    low = jnp.bitwise_and(row, 63).astype(jnp.float32)
    values = jnp.concatenate([hot_f * high, hot_f * low], axis=0).astype(jnp.bfloat16)
    table = dot(values, of_rank, ((1,), (1,)))
    return (table[:n] * 64.0 + table[n:]).astype(jnp.int32) - 1


def slot_row(table, n):
    slots = n * CAP
    shifted = table + 1
    high = lax.shift_right_arithmetic(shifted, 6).astype(jnp.float32)
    low = jnp.bitwise_and(shifted, 63).astype(jnp.float32)
    parts = jnp.concatenate([high, low], axis=0).astype(jnp.bfloat16)
    lane = jnp.bitwise_and(iota((LANES, slots), 1), CAP - 1)
    spread = jnp.where(iota((LANES, slots), 0) == lane, 1.0, 0.0).astype(jnp.bfloat16)
    wide = dot(parts, spread)
    both = wide[:n] * 64.0 + wide[n:]
    mine = lax.shift_right_arithmetic(iota((n, slots), 1), 5) == iota((n, slots), 0)
    row = jnp.sum(jnp.where(mine, both, 0.0), axis=0, keepdims=True)
    return row.astype(jnp.int32) - 1


def kernel(
    n, group,
    ids_ref, q_hbm, pos_hbm, pas_hbm,
    loss_ref, pas, pos,
    q, send, got, ret, big, wt,
    req, want, bias, wrow, tops, sums, prow, crow,
    load_s, rq_s, rq_r, f_s, f_r, r_s, r_r, wx_s, wx_r, sw_s, sw_r, free_s, near_s,
):
    me, core = lax.axis_index("idx"), lax.axis_index("enc")
    queries, depth = q.shape
    shard_rows = pas.shape[0]
    slots = n * CAP
    chunk = group * CAP
    chunks = n // group
    scale = 3.0 / math.sqrt(depth)
    factor = LSCALE * scale
    cut = depth // 2
    steps = [
        (1 << k) * (1 - 2 * lax.rem(lax.div(me, 1 << k), 2))
        for k in range(int(math.log2(n)))
    ]

    def partner(c, j):
        bits = place_bits(c, j, n, group)
        there = me
        for bit, step in zip(bits, steps):
            if isinstance(bit, int):
                there = there + step if bit else there
            else:
                there = there + bit * step
        return there

    def of_chunk(c, work):
        for j in range(group):
            if j == 0:
                @pl.when(c > 0)
                def _():
                    work(c * group + j, partner(c, j))
            else:
                work(c * group + j, partner(c, j))

    def loop(start, stop, body):
        def step(c, carry):
            body(c)
            return carry

        lax.fori_loop(start, stop, step, 0)

    def each(work):
        loop(0, chunks, lambda c: of_chunk(c, work))

    def part(c):
        return pl.ds(pl.multiple_of(c * chunk, chunk), chunk)

    def rows_at(p):
        return pl.ds(pl.multiple_of(p * CAP, CAP), CAP)

    def pair(c):
        return pl.ds(pl.multiple_of(c * 2 * chunk, 2 * chunk), 2 * chunk)

    def home(p, whose):
        c, j = lax.div(p, group), lax.rem(p, group)
        return pl.ds(pl.multiple_of((c * 2 + whose) * chunk + j * CAP, CAP), CAP)

    def ask(p, there):
        return pltpu.make_async_remote_copy(
            src_ref=req.at[p], dst_ref=want.at[p], send_sem=rq_s.at[p],
            recv_sem=rq_r.at[p], device_id=(there, core), device_id_type=MESH)

    def fetch(p, there):
        return pltpu.make_async_remote_copy(
            src_ref=send.at[rows_at(p)], dst_ref=got.at[rows_at(p)], send_sem=f_s.at[p],
            recv_sem=f_r.at[p], device_id=(there, core), device_id_type=MESH)

    def give(p, there, side):
        return pltpu.make_async_remote_copy(
            src_ref=send.at[rows_at(p), pl.ds(pl.multiple_of(side * cut, cut), cut)],
            dst_ref=ret.at[home(p, core)], send_sem=r_s.at[side, p],
            recv_sem=r_r.at[core, p], device_id=(there, side), device_id_type=MESH)

    def given(p, whose):
        return pltpu.make_async_remote_copy(
            src_ref=ret.at[home(p, whose)], dst_ref=ret.at[home(p, whose)],
            send_sem=r_s.at[whose, p], recv_sem=r_r.at[whose, p],
            device_id=(me, 1 - core), device_id_type=MESH)

    def pass_row(whose):
        return pltpu.make_async_remote_copy(
            src_ref=wrow.at[whose], dst_ref=wrow.at[whose], send_sem=wx_s, recv_sem=wx_r,
            device_id=(me, 1 - core), device_id_type=MESH)

    loads = [
        pltpu.make_async_copy(src, dst, load_s.at[k])
        for k, (src, dst) in enumerate([(pas_hbm, pas), (q_hbm, q), (pos_hbm, pos)])
    ]

    barrier = pltpu.get_barrier_semaphore()
    axes = [steps[k : k + 2] for k in range(0, len(steps), 2)]

    def along(axis):
        return [
            sum([s for k, s in enumerate(axis) if far >> k & 1], me)
            for far in range(1, 1 << len(axis))
        ]

    def greet(semaphore, axis):
        for there in along(axis):
            pl.semaphore_signal(
                semaphore, inc=1, device_id=(there, core), device_id_type=MESH)

    for axis in axes:
        greet(barrier, axis)
    pl.semaphore_signal(barrier, inc=1, device_id=(me, 1 - core), device_id_type=MESH)
    for load in loads:
        load.start()
    table = request_table(ids_ref[...], me, n, shard_rows)
    for p in range(n):
        req[p] = table[p : p + 1]
    want[0] = table[0:1]
    pl.semaphore_wait(barrier, 1 + sum(len(along(axis)) for axis in axes))
    for k, axis in enumerate(axes[1:]):
        greet(near_s.at[k], axis)
        pl.semaphore_wait(near_s.at[k], len(along(axis)))

    each(lambda p, there: ask(p, there).start())

    def columns(rows, into, change):
        rows_t = turned(rows)
        for p in range(n):
            into[p * CAP : (p + 1) * CAP, :] = jnp.broadcast_to(
                change(rows_t[:CAP, p : p + 1]), (CAP, LANES))

    loads[0].wait()

    def gather(c):
        asked = turned(want[pl.ds(c * group, group), 0, :])
        w = jnp.concatenate(
            [jnp.broadcast_to(asked[:CAP, j : j + 1], (CAP, LANES)) for j in range(group)],
            axis=0)
        lane = iota((chunk, LANES), 1)
        hot = jnp.concatenate(
            [jnp.where(w == lane + k, 1.0, 0.0).astype(jnp.bfloat16)
             for k in range(0, shard_rows, LANES)], axis=1)
        send[part(c), :] = dot(hot, pas[...]).astype(jnp.bfloat16)

    def gather_and_send(c):
        of_chunk(c, lambda p, there: ask(p, there).wait_recv())
        gather(c)
        of_chunk(c, lambda p, there: fetch(p, there).start())

    loop(0, chunks, gather_and_send)
    got[0:CAP, :] = send[0:CAP, :]

    block = min(256, queries)
    wide = min(512, queries)

    def block_at(b):
        return pl.ds(pl.multiple_of(b * block, block), block)

    def other_form():
        wrow[core] = slot_row(want[:, 0, :], n)

    def mask():
        columns(req[:, 0, :], bias, lambda x: jnp.where(x >= 0, 0.0, NONE))

    def positive(b):
        both = q[block_at(b), :].astype(jnp.float32) * pos[block_at(b), :].astype(jnp.float32)
        total = both[:, :LANES]
        for k in range(LANES, depth, LANES):
            total = total + both[:, k : k + LANES]
        prow[:, block_at(b)] = scale * jnp.sum(total.T, axis=0, keepdims=True)

    def turn(b):
        wt[0:depth, block_at(b)] = q[block_at(b), :].T

    other_form()
    pass_row(core).start()
    mask()
    loads[1].wait()
    loads[2].wait()
    loop(0, queries // block, positive)
    loop(0, queries // block, turn)
    each(lambda p, there: ask(p, there).wait_send())

    power = scale * math.log2(math.e)

    def logits(c):
        def product(at):
            return dot(got[part(c), :], wt[0:depth, at : at + wide])

        ahead = product(0)
        for at in range(0, queries, wide):
            x = ahead
            if at + wide < queries:
                ahead = product(at + wide)
            x = x + jnp.concatenate([bias[part(c), :]] * (wide // LANES), axis=1)
            top = jnp.max(x, axis=0, keepdims=True)
            x = jnp.exp2(power * (x - top))
            big[part(c), at : at + wide] = x
            tops[c, :, at : at + wide] = scale * top
            sums[c, :, at : at + wide] = jnp.sum(x, axis=0, keepdims=True)

    def receive(c):
        of_chunk(c, lambda p, there: fetch(p, there).wait_recv())

        logits(c)

    loop(0, chunks, receive)

    def totals():
        pos_logit = prow[...]
        top = pos_logit
        for c in range(chunks):
            top = jnp.maximum(top, tops[c])
        pos_exp = jnp.exp(pos_logit - top)
        total = pos_exp
        for c in range(chunks):
            total = total + sums[c] * jnp.exp(tops[c] - top)
        for c in range(chunks):
            tops[c] = jnp.exp(tops[c] - top) * (factor / total)
        crow[...] = factor * (pos_exp / total - 1.0)
        loss_ref[...] = top + jnp.log(total) - pos_logit

    totals()

    def row_grads(c):
        wt[part(c), :] = (big[part(c), :] * tops[c]).astype(jnp.bfloat16)
        send[part(c), :] = dot(wt[part(c), :], q[...]).astype(jnp.bfloat16)

    def return_rows(c):
        of_chunk(c, lambda p, there: fetch(p, there).wait_send())
        row_grads(c)

        @pl.when(c == 0)
        def _():
            give(0, me, 1 - core).start()

        def both(p, there):
            give(p, there, 0).start()
            give(p, there, 1).start()

        of_chunk(c, both)

    def wide_at(b):
        return pl.ds(pl.multiple_of(b * wide, wide), wide)

    def query_grads(b):
        g = dot(wt[:, wide_at(b)], got[...], ((0,), (0,)))
        coef = jnp.broadcast_to(crow[:, wide_at(b)], (LANES, wide)).T
        coef = jnp.concatenate([coef] * (depth // LANES), axis=1)
        g = g + coef * pos[wide_at(b), :].astype(jnp.float32)
        pas[wide_at(b), :] = g.astype(jnp.bfloat16)

    tall = min(512, shard_rows)

    def tall_at(b):
        return pl.ds(pl.multiple_of(b * tall, tall), tall)

    def clear(b):
        big[tall_at(b), 0:cut] = jnp.zeros((tall, cut), jnp.float32)

    loop(0, chunks, return_rows)
    mine = pl.ds(pl.multiple_of(core * cut, cut), cut)
    ret[home(0, core), :] = send[0:CAP, mine]
    loop(0, queries // wide, query_grads)
    pl.semaphore_signal(free_s, inc=1, device_id=(me, 1 - core), device_id_type=MESH)
    loop(0, shard_rows // tall, clear)
    pass_row(1 - core).wait_recv()

    def added(c, b):
        here = iota((tall, chunk), 0) + b * tall
        hot = jnp.concatenate(
            [jnp.where(here == wrow[whose, :, part(c)], 1.0, 0.0).astype(jnp.bfloat16)
             for whose in range(2)], axis=1)
        return big[tall_at(b), 0:cut] + dot(hot, ret[pair(c), :])

    def add_up(c):
        for b in range(shard_rows // tall):
            big[tall_at(b), 0:cut] = added(c, b)

    def add_last(b):
        pos[tall_at(b), mine] = added(chunks - 1, b).astype(jnp.bfloat16)

    def swap(b, side):
        block = pos.at[tall_at(b), pl.ds(pl.multiple_of(side * cut, cut), cut)]
        return pltpu.make_async_remote_copy(
            src_ref=block, dst_ref=block, send_sem=sw_s.at[b], recv_sem=sw_r.at[b],
            device_id=(me, 1 - core), device_id_type=MESH)

    def take(c):
        def both(p, there):
            given(p, 0).wait_recv()
            given(p, 1).wait_recv()

        of_chunk(c, both)

    def collect(c):
        take(c)
        add_up(c)

    given(0, 1 - core).wait_recv()
    loop(0, chunks - 1, collect)
    take(chunks - 1)
    pl.semaphore_wait(free_s, 1)
    for b in range(shard_rows // tall):
        add_last(b)
        swap(b, core).start()

    def sent(p, there):
        give(p, there, 0).wait_send()
        give(p, there, 1).wait_send()

    each(sent)
    give(0, me, 1 - core).wait_send()
    pass_row(core).wait_send()
    for b in range(shard_rows // tall):
        swap(b, core).wait_send()
        swap(b, 1 - core).wait_recv()


def local(group, queries, positives, passages, negatives):
    n = lax.axis_size("idx")
    count, depth = queries.shape
    shard_rows = passages.shape[0]
    slots = n * CAP
    chunks = n // group
    any_space = pl.BlockSpec(memory_space=pl.ANY)
    vmem = pl.BlockSpec(memory_space=pltpu.VMEM)
    dma = pltpu.SemaphoreType.DMA
    bf16, f32 = jnp.bfloat16, jnp.float32
    loss, grad_q, grad_p = pl.pallas_call(
        functools.partial(kernel, n, group),
        out_shape=(
            jax.ShapeDtypeStruct((1, count), f32),
            pltpu.VMEM((count, depth), bf16),
            pltpu.VMEM((shard_rows, depth), bf16),
        ),
        in_specs=[vmem, any_space, any_space, any_space],
        out_specs=(vmem, vmem, vmem),
        scratch_shapes=[
            pltpu.VMEM((count, depth), bf16),
            pltpu.VMEM((slots, depth), bf16),
            pltpu.VMEM((slots, depth), bf16),
            pltpu.VMEM((2 * slots, depth // 2), bf16),
            pltpu.VMEM((slots, count), f32),
            pltpu.VMEM((slots, count), bf16),
            pltpu.VMEM((n, 1, LANES), jnp.int32),
            pltpu.VMEM((n, 1, LANES), jnp.int32),
            pltpu.VMEM((slots, LANES), f32),
            pltpu.VMEM((2, 1, slots), jnp.int32),
            pltpu.VMEM((chunks, 1, count), f32),
            pltpu.VMEM((chunks, 1, count), f32),
            pltpu.VMEM((1, count), f32),
            pltpu.VMEM((1, count), f32),
            dma((3,)),
            dma((n,)), dma((n,)),
            dma((n,)), dma((n,)),
            dma((2, n)), dma((2, n)),
            dma, dma,
            dma((shard_rows // min(512, shard_rows),)),
            dma((shard_rows // min(512, shard_rows),)),
            pltpu.SemaphoreType.REGULAR,
            pltpu.SemaphoreType.REGULAR((2,)),
        ],
        compiler_params=pltpu.CompilerParams(
            collective_id=0, has_side_effects=True, vmem_limit_bytes=52 << 20
        ),
        cost_estimate=pl.CostEstimate(
            flops=12 * slots * count * depth, bytes_accessed=20 * count * depth,
            transcendentals=slots * count,
        ),
    )(negatives.reshape(1, -1), queries, positives, passages)
    return loss.reshape(-1), grad_q, grad_p


def solution(mesh, group=8):
    placed = (
        P(("idx", "enc"), None),
        P(("idx", "enc"), None),
        P("idx", None),
        P(("idx", "enc"), None),
    )
    return jax.shard_map(
        functools.partial(local, group),
        mesh=mesh,
        in_specs=placed,
        out_specs=(P(("idx", "enc")), P(("idx", "enc"), None), P("idx", None)),
        check_vma=False,
    )
```

```python
import functools
import math

import jax
import jax.numpy as jnp
from jax import lax
from jax.experimental import pallas as pl
from jax.experimental.pallas import tpu as pltpu
from jax.sharding import PartitionSpec as P

LSCALE = 32
CAP = 32
LANES = 128
MESH = pl.DeviceIdType.MESH
NONE = -1e30


def flip(u, v):
    if isinstance(u, int):
        return 1 - v if u else v
    return u + v - 2 * u * v


def place_bits(c, j, n, group):
    low = int(math.log2(group))
    count = int(math.log2(n))
    p = [(j >> k) & 1 for k in range(low)]
    p += [lax.rem(lax.div(c, 1 << k), 2) for k in range(count - low)]
    if n != 64:
        return p
    t0, t1, b0, b1, a0, a1 = p
    return [t0, t1, flip(t0, a0), flip(t1, a1), flip(t0, b0), flip(t1, b1)]


def place_of(distance, n):
    if n != 64:
        return distance
    z, x, y = distance & 3, (distance >> 2) & 3, (distance >> 4) & 3
    return ((x ^ z) << 4) + ((y ^ z) << 2) + z


def iota(shape, dim):
    return lax.broadcasted_iota(jnp.int32, shape, dim)


def dot(a, b, dims=((1,), (0,))):
    return lax.dot_general(a, b, (dims, ((), ())), preferred_element_type=jnp.float32)


def turned(rows):
    m = rows.shape[0]
    if m < LANES:
        rows = jnp.concatenate([rows, jnp.zeros((LANES - m, LANES), rows.dtype)], axis=0)
    return rows.T


def request_table(ids, me, n, shard_rows):
    slots = ids.shape[1]
    shift = int(math.log2(shard_rows))
    live = ids >= 0
    place = place_of(jnp.bitwise_xor(lax.shift_right_arithmetic(ids, shift), me), n)
    place = jnp.where(live, place, -1)
    row = jnp.bitwise_and(ids, shard_rows - 1) + 1
    hot = iota((n, slots), 0) == place
    hot_f = jnp.where(hot, 1.0, 0.0)
    width = min(256, slots)
    before = jnp.where(
        iota((width, width), 0) < iota((width, width), 1), 1.0, 0.0
    ).astype(jnp.bfloat16)
    carry = jnp.zeros((n, 1), jnp.float32)
    ranks = []
    for at in range(0, slots, width):
        part = hot_f[:, at : at + width]
        ahead = dot(part.astype(jnp.bfloat16), before) + carry
        ranks.append(jnp.sum(part * ahead, axis=0, keepdims=True))
        carry = carry + jnp.sum(part, axis=1, keepdims=True)
    rank = jnp.concatenate(ranks, axis=1).astype(jnp.int32)
    of_rank = jnp.where(iota((LANES, slots), 0) == rank, 1.0, 0.0).astype(jnp.bfloat16)
    high = lax.shift_right_arithmetic(row, 6).astype(jnp.float32)
    low = jnp.bitwise_and(row, 63).astype(jnp.float32)
    values = jnp.concatenate([hot_f * high, hot_f * low], axis=0).astype(jnp.bfloat16)
    table = dot(values, of_rank, ((1,), (1,)))
    return (table[:n] * 64.0 + table[n:]).astype(jnp.int32) - 1


def slot_row(table, n):
    slots = n * CAP
    shifted = table + 1
    high = lax.shift_right_arithmetic(shifted, 6).astype(jnp.float32)
    low = jnp.bitwise_and(shifted, 63).astype(jnp.float32)
    parts = jnp.concatenate([high, low], axis=0).astype(jnp.bfloat16)
    lane = jnp.bitwise_and(iota((LANES, slots), 1), CAP - 1)
    spread = jnp.where(iota((LANES, slots), 0) == lane, 1.0, 0.0).astype(jnp.bfloat16)
    wide = dot(parts, spread)
    both = wide[:n] * 64.0 + wide[n:]
    mine = lax.shift_right_arithmetic(iota((n, slots), 1), 5) == iota((n, slots), 0)
    row = jnp.sum(jnp.where(mine, both, 0.0), axis=0, keepdims=True)
    return row.astype(jnp.int32) - 1


def kernel(
    n, group,
    ids_ref, q_hbm, pos_hbm, pas_hbm,
    loss_ref, pas, pos,
    q, send, got, ret, big, wt,
    req, want, bias, wrow, tops, sums, prow, crow,
    load_s, rq_s, rq_r, f_s, f_r, r_s, r_r, wx_s, wx_r, sw_s, sw_r, free_s,
):
    me, core = lax.axis_index("idx"), lax.axis_index("enc")
    queries, depth = q.shape
    shard_rows = pas.shape[0]
    slots = n * CAP
    chunk = group * CAP
    chunks = n // group
    scale = 3.0 / math.sqrt(depth)
    factor = LSCALE * scale
    cut = depth // 2
    steps = [
        (1 << k) * (1 - 2 * lax.rem(lax.div(me, 1 << k), 2))
        for k in range(int(math.log2(n)))
    ]

    def partner(c, j):
        bits = place_bits(c, j, n, group)
        there = me
        for bit, step in zip(bits, steps):
            if isinstance(bit, int):
                there = there + step if bit else there
            else:
                there = there + bit * step
        return there

    def of_chunk(c, work):
        for j in range(group):
            if j == 0:
                @pl.when(c > 0)
                def _():
                    work(c * group + j, partner(c, j))
            else:
                work(c * group + j, partner(c, j))

    def loop(start, stop, body):
        def step(c, carry):
            body(c)
            return carry

        lax.fori_loop(start, stop, step, 0)

    def each(work):
        loop(0, chunks, lambda c: of_chunk(c, work))

    def part(c):
        return pl.ds(pl.multiple_of(c * chunk, chunk), chunk)

    def rows_at(p):
        return pl.ds(pl.multiple_of(p * CAP, CAP), CAP)

    def pair(c):
        return pl.ds(pl.multiple_of(c * 2 * chunk, 2 * chunk), 2 * chunk)

    def home(p, whose):
        c, j = lax.div(p, group), lax.rem(p, group)
        return pl.ds(pl.multiple_of((c * 2 + whose) * chunk + j * CAP, CAP), CAP)

    def ask(p, there):
        return pltpu.make_async_remote_copy(
            src_ref=req.at[p], dst_ref=want.at[p], send_sem=rq_s.at[p],
            recv_sem=rq_r.at[p], device_id=(there, core), device_id_type=MESH)

    def fetch(p, there):
        return pltpu.make_async_remote_copy(
            src_ref=send.at[rows_at(p)], dst_ref=got.at[rows_at(p)], send_sem=f_s.at[p],
            recv_sem=f_r.at[p], device_id=(there, core), device_id_type=MESH)

    def give(p, there, side):
        return pltpu.make_async_remote_copy(
            src_ref=send.at[rows_at(p), pl.ds(pl.multiple_of(side * cut, cut), cut)],
            dst_ref=ret.at[home(p, core)], send_sem=r_s.at[side, p],
            recv_sem=r_r.at[core, p], device_id=(there, side), device_id_type=MESH)

    def given(p, whose):
        return pltpu.make_async_remote_copy(
            src_ref=ret.at[home(p, whose)], dst_ref=ret.at[home(p, whose)],
            send_sem=r_s.at[whose, p], recv_sem=r_r.at[whose, p],
            device_id=(me, 1 - core), device_id_type=MESH)

    def pass_row(whose):
        return pltpu.make_async_remote_copy(
            src_ref=wrow.at[whose], dst_ref=wrow.at[whose], send_sem=wx_s, recv_sem=wx_r,
            device_id=(me, 1 - core), device_id_type=MESH)

    loads = [
        pltpu.make_async_copy(src, dst, load_s.at[k])
        for k, (src, dst) in enumerate([(pas_hbm, pas), (q_hbm, q), (pos_hbm, pos)])
    ]

    barrier = pltpu.get_barrier_semaphore()
    each(lambda p, there: pl.semaphore_signal(
        barrier, inc=1, device_id=(there, core), device_id_type=MESH))
    pl.semaphore_signal(barrier, inc=1, device_id=(me, 1 - core), device_id_type=MESH)
    for load in loads:
        load.start()
    table = request_table(ids_ref[...], me, n, shard_rows)
    for p in range(n):
        req[p] = table[p : p + 1]
    want[0] = table[0:1]
    pl.semaphore_wait(barrier, n)

    each(lambda p, there: ask(p, there).start())

    def columns(rows, into, change):
        rows_t = turned(rows)
        for p in range(n):
            into[p * CAP : (p + 1) * CAP, :] = jnp.broadcast_to(
                change(rows_t[:CAP, p : p + 1]), (CAP, LANES))

    loads[0].wait()

    def gather(c):
        asked = turned(want[pl.ds(c * group, group), 0, :])
        w = jnp.concatenate(
            [jnp.broadcast_to(asked[:CAP, j : j + 1], (CAP, LANES)) for j in range(group)],
            axis=0)
        lane = iota((chunk, LANES), 1)
        hot = jnp.concatenate(
            [jnp.where(w == lane + k, 1.0, 0.0).astype(jnp.bfloat16)
             for k in range(0, shard_rows, LANES)], axis=1)
        send[part(c), :] = dot(hot, pas[...]).astype(jnp.bfloat16)

    def gather_and_send(c):
        of_chunk(c, lambda p, there: ask(p, there).wait_recv())
        gather(c)
        of_chunk(c, lambda p, there: fetch(p, there).start())

    loop(0, chunks, gather_and_send)
    got[0:CAP, :] = send[0:CAP, :]

    block = min(256, queries)
    wide = min(512, queries)

    def block_at(b):
        return pl.ds(pl.multiple_of(b * block, block), block)

    def other_form():
        wrow[core] = slot_row(want[:, 0, :], n)

    def mask():
        columns(req[:, 0, :], bias, lambda x: jnp.where(x >= 0, 0.0, NONE))

    def positive(b):
        both = q[block_at(b), :].astype(jnp.float32) * pos[block_at(b), :].astype(jnp.float32)
        total = both[:, :LANES]
        for k in range(LANES, depth, LANES):
            total = total + both[:, k : k + LANES]
        prow[:, block_at(b)] = scale * jnp.sum(total.T, axis=0, keepdims=True)

    def turn(b):
        wt[0:depth, block_at(b)] = q[block_at(b), :].T

    other_form()
    pass_row(core).start()
    mask()
    loads[1].wait()
    loads[2].wait()
    loop(0, queries // block, positive)
    loop(0, queries // block, turn)
    each(lambda p, there: ask(p, there).wait_send())

    power = scale * math.log2(math.e)

    def logits(c):
        def product(at):
            return dot(got[part(c), :], wt[0:depth, at : at + wide])

        ahead = product(0)
        for at in range(0, queries, wide):
            x = ahead
            if at + wide < queries:
                ahead = product(at + wide)
            x = x + jnp.concatenate([bias[part(c), :]] * (wide // LANES), axis=1)
            top = jnp.max(x, axis=0, keepdims=True)
            x = jnp.exp2(power * (x - top))
            big[part(c), at : at + wide] = x
            tops[c, :, at : at + wide] = scale * top
            sums[c, :, at : at + wide] = jnp.sum(x, axis=0, keepdims=True)

    def receive(c):
        of_chunk(c, lambda p, there: fetch(p, there).wait_recv())

        logits(c)

    loop(0, chunks, receive)

    def totals():
        pos_logit = prow[...]
        top = pos_logit
        for c in range(chunks):
            top = jnp.maximum(top, tops[c])
        pos_exp = jnp.exp(pos_logit - top)
        total = pos_exp
        for c in range(chunks):
            total = total + sums[c] * jnp.exp(tops[c] - top)
        for c in range(chunks):
            tops[c] = jnp.exp(tops[c] - top) * (factor / total)
        crow[...] = factor * (pos_exp / total - 1.0)
        loss_ref[...] = top + jnp.log(total) - pos_logit

    totals()

    def row_grads(c):
        wt[part(c), :] = (big[part(c), :] * tops[c]).astype(jnp.bfloat16)
        send[part(c), :] = dot(wt[part(c), :], q[...]).astype(jnp.bfloat16)

    def return_rows(c):
        of_chunk(c, lambda p, there: fetch(p, there).wait_send())
        row_grads(c)

        @pl.when(c == 0)
        def _():
            give(0, me, 1 - core).start()

        def both(p, there):
            give(p, there, 0).start()
            give(p, there, 1).start()

        of_chunk(c, both)

    def wide_at(b):
        return pl.ds(pl.multiple_of(b * wide, wide), wide)

    def query_grads(b):
        g = dot(wt[:, wide_at(b)], got[...], ((0,), (0,)))
        coef = jnp.broadcast_to(crow[:, wide_at(b)], (LANES, wide)).T
        coef = jnp.concatenate([coef] * (depth // LANES), axis=1)
        g = g + coef * pos[wide_at(b), :].astype(jnp.float32)
        pas[wide_at(b), :] = g.astype(jnp.bfloat16)

    tall = min(512, shard_rows)

    def tall_at(b):
        return pl.ds(pl.multiple_of(b * tall, tall), tall)

    def clear(b):
        big[tall_at(b), 0:cut] = jnp.zeros((tall, cut), jnp.float32)

    loop(0, chunks, return_rows)
    mine = pl.ds(pl.multiple_of(core * cut, cut), cut)
    ret[home(0, core), :] = send[0:CAP, mine]
    loop(0, queries // wide, query_grads)
    pl.semaphore_signal(free_s, inc=1, device_id=(me, 1 - core), device_id_type=MESH)
    loop(0, shard_rows // tall, clear)
    pass_row(1 - core).wait_recv()

    def added(c, b):
        here = iota((tall, chunk), 0) + b * tall
        hot = jnp.concatenate(
            [jnp.where(here == wrow[whose, :, part(c)], 1.0, 0.0).astype(jnp.bfloat16)
             for whose in range(2)], axis=1)
        return big[tall_at(b), 0:cut] + dot(hot, ret[pair(c), :])

    def add_up(c):
        for b in range(shard_rows // tall):
            big[tall_at(b), 0:cut] = added(c, b)

    def add_last(b):
        pos[tall_at(b), mine] = added(chunks - 1, b).astype(jnp.bfloat16)

    def swap(b, side):
        block = pos.at[tall_at(b), pl.ds(pl.multiple_of(side * cut, cut), cut)]
        return pltpu.make_async_remote_copy(
            src_ref=block, dst_ref=block, send_sem=sw_s.at[b], recv_sem=sw_r.at[b],
            device_id=(me, 1 - core), device_id_type=MESH)

    def take(c):
        def both(p, there):
            given(p, 0).wait_recv()
            given(p, 1).wait_recv()

        of_chunk(c, both)

    def collect(c):
        take(c)
        add_up(c)

    given(0, 1 - core).wait_recv()
    loop(0, chunks - 1, collect)
    take(chunks - 1)
    pl.semaphore_wait(free_s, 1)
    for b in range(shard_rows // tall):
        add_last(b)
        swap(b, core).start()

    def sent(p, there):
        give(p, there, 0).wait_send()
        give(p, there, 1).wait_send()

    each(sent)
    give(0, me, 1 - core).wait_send()
    pass_row(core).wait_send()
    for b in range(shard_rows // tall):
        swap(b, core).wait_send()
        swap(b, 1 - core).wait_recv()


def hand_over(loss, grad_q, grad_p, loss_out, grad_q_out, grad_p_out, done):
    moves = [
        pltpu.make_async_copy(src, dst, done.at[k])
        for k, (src, dst) in enumerate(
            [(grad_p, grad_p_out), (grad_q, grad_q_out), (loss, loss_out)])
    ]
    for move in moves:
        move.start()
    for move in moves:
        move.wait()


def local(group, queries, positives, passages, negatives):
    n = lax.axis_size("idx")
    count, depth = queries.shape
    shard_rows = passages.shape[0]
    slots = n * CAP
    chunks = n // group
    any_space = pl.BlockSpec(memory_space=pl.ANY)
    vmem = pl.BlockSpec(memory_space=pltpu.VMEM)
    dma = pltpu.SemaphoreType.DMA
    bf16, f32 = jnp.bfloat16, jnp.float32
    loss, grad_q, grad_p = pl.pallas_call(
        functools.partial(kernel, n, group),
        out_shape=(
            pltpu.VMEM((1, count), f32),
            pltpu.VMEM((count, depth), bf16),
            pltpu.VMEM((shard_rows, depth), bf16),
        ),
        in_specs=[vmem, any_space, any_space, any_space],
        out_specs=(vmem, vmem, vmem),
        scratch_shapes=[
            pltpu.VMEM((count, depth), bf16),
            pltpu.VMEM((slots, depth), bf16),
            pltpu.VMEM((slots, depth), bf16),
            pltpu.VMEM((2 * slots, depth // 2), bf16),
            pltpu.VMEM((slots, count), f32),
            pltpu.VMEM((slots, count), bf16),
            pltpu.VMEM((n, 1, LANES), jnp.int32),
            pltpu.VMEM((n, 1, LANES), jnp.int32),
            pltpu.VMEM((slots, LANES), f32),
            pltpu.VMEM((2, 1, slots), jnp.int32),
            pltpu.VMEM((chunks, 1, count), f32),
            pltpu.VMEM((chunks, 1, count), f32),
            pltpu.VMEM((1, count), f32),
            pltpu.VMEM((1, count), f32),
            dma((3,)),
            dma((n,)), dma((n,)),
            dma((n,)), dma((n,)),
            dma((2, n)), dma((2, n)),
            dma, dma,
            dma((shard_rows // min(512, shard_rows),)),
            dma((shard_rows // min(512, shard_rows),)),
            pltpu.SemaphoreType.REGULAR,
        ],
        compiler_params=pltpu.CompilerParams(
            collective_id=0, has_side_effects=True, vmem_limit_bytes=52 << 20
        ),
        cost_estimate=pl.CostEstimate(
            flops=12 * slots * count * depth, bytes_accessed=20 * count * depth,
            transcendentals=slots * count,
        ),
    )(negatives.reshape(1, -1), queries, positives, passages)
    loss, grad_q, grad_p = pl.pallas_call(
        hand_over,
        out_shape=(
            jax.ShapeDtypeStruct((1, count), f32),
            jax.ShapeDtypeStruct((count, depth), bf16),
            jax.ShapeDtypeStruct((shard_rows, depth), bf16),
        ),
        in_specs=[any_space] * 3,
        out_specs=(any_space,) * 3,
        scratch_shapes=[dma((3,))],
        compiler_params=pltpu.CompilerParams(vmem_limit_bytes=1 << 20),
    )(loss, grad_q, grad_p)
    return loss.reshape(-1), grad_q, grad_p


def solution(mesh, group=8):
    placed = (
        P(("idx", "enc"), None),
        P(("idx", "enc"), None),
        P("idx", None),
        P(("idx", "enc"), None),
    )
    return jax.shard_map(
        functools.partial(local, group),
        mesh=mesh,
        in_specs=placed,
        out_specs=(P(("idx", "enc")), P(("idx", "enc"), None), P("idx", None)),
        check_vma=False,
    )
```

```python
import functools
import math

import jax
import jax.numpy as jnp
from jax import lax
from jax.experimental import pallas as pl
from jax.experimental.pallas import tpu as pltpu
from jax.sharding import PartitionSpec as P

LSCALE = 32
CAP = 32
LANES = 128
MESH = pl.DeviceIdType.MESH
NONE = -1e30


def flip(u, v):
    if isinstance(u, int):
        return 1 - v if u else v
    return u + v - 2 * u * v


def place_bits(c, j, n, group):
    low = int(math.log2(group))
    count = int(math.log2(n))
    p = [(j >> k) & 1 for k in range(low)]
    p += [lax.rem(lax.div(c, 1 << k), 2) for k in range(count - low)]
    if n != 64:
        return p
    t0, t1, b0, b1, a0, a1 = p
    return [t0, t1, flip(t0, a0), flip(t1, a1), flip(t0, b0), flip(t1, b1)]


def place_of(distance, n):
    if n != 64:
        return distance
    z, x, y = distance & 3, (distance >> 2) & 3, (distance >> 4) & 3
    return ((x ^ z) << 4) + ((y ^ z) << 2) + z


def iota(shape, dim):
    return lax.broadcasted_iota(jnp.int32, shape, dim)


def dot(a, b, dims=((1,), (0,))):
    return lax.dot_general(a, b, (dims, ((), ())), preferred_element_type=jnp.float32)


def turned(rows):
    m = rows.shape[0]
    if m < LANES:
        rows = jnp.concatenate([rows, jnp.zeros((LANES - m, LANES), rows.dtype)], axis=0)
    return rows.T


def request_table(ids, me, n, shard_rows):
    slots = ids.shape[1]
    shift = int(math.log2(shard_rows))
    live = ids >= 0
    place = place_of(jnp.bitwise_xor(lax.shift_right_arithmetic(ids, shift), me), n)
    place = jnp.where(live, place, -1)
    row = jnp.bitwise_and(ids, shard_rows - 1) + 1
    hot = iota((n, slots), 0) == place
    hot_f = jnp.where(hot, 1.0, 0.0)
    width = min(256, slots)
    before = jnp.where(
        iota((width, width), 0) < iota((width, width), 1), 1.0, 0.0
    ).astype(jnp.bfloat16)
    carry = jnp.zeros((n, 1), jnp.float32)
    ranks = []
    for at in range(0, slots, width):
        part = hot_f[:, at : at + width]
        ahead = dot(part.astype(jnp.bfloat16), before) + carry
        ranks.append(jnp.sum(part * ahead, axis=0, keepdims=True))
        carry = carry + jnp.sum(part, axis=1, keepdims=True)
    rank = jnp.concatenate(ranks, axis=1).astype(jnp.int32)
    of_rank = jnp.where(iota((LANES, slots), 0) == rank, 1.0, 0.0).astype(jnp.bfloat16)
    high = lax.shift_right_arithmetic(row, 6).astype(jnp.float32)
    low = jnp.bitwise_and(row, 63).astype(jnp.float32)
    values = jnp.concatenate([hot_f * high, hot_f * low], axis=0).astype(jnp.bfloat16)
    table = dot(values, of_rank, ((1,), (1,)))
    return (table[:n] * 64.0 + table[n:]).astype(jnp.int32) - 1


def slot_row(table, n):
    slots = n * CAP
    shifted = table + 1
    high = lax.shift_right_arithmetic(shifted, 6).astype(jnp.float32)
    low = jnp.bitwise_and(shifted, 63).astype(jnp.float32)
    parts = jnp.concatenate([high, low], axis=0).astype(jnp.bfloat16)
    lane = jnp.bitwise_and(iota((LANES, slots), 1), CAP - 1)
    spread = jnp.where(iota((LANES, slots), 0) == lane, 1.0, 0.0).astype(jnp.bfloat16)
    wide = dot(parts, spread)
    both = wide[:n] * 64.0 + wide[n:]
    mine = lax.shift_right_arithmetic(iota((n, slots), 1), 5) == iota((n, slots), 0)
    row = jnp.sum(jnp.where(mine, both, 0.0), axis=0, keepdims=True)
    return row.astype(jnp.int32) - 1


def kernel(
    n, group,
    ids_ref, q_hbm, pos_hbm, pas_hbm,
    loss_ref, pas, pos,
    q, send, got, ret, big, wt,
    req, want, bias, wrow, tops, sums, prow, crow,
    load_s, rq_s, rq_r, f_s, f_r, r_s, r_r, wx_s, wx_r, sw_s, sw_r, free_s,
):
    me, core = lax.axis_index("idx"), lax.axis_index("enc")
    queries, depth = q.shape
    shard_rows = pas.shape[0]
    slots = n * CAP
    chunk = group * CAP
    chunks = n // group
    scale = 3.0 / math.sqrt(depth)
    factor = LSCALE * scale
    cut = depth // 2
    steps = [
        (1 << k) * (1 - 2 * lax.rem(lax.div(me, 1 << k), 2))
        for k in range(int(math.log2(n)))
    ]

    def partner(c, j):
        bits = place_bits(c, j, n, group)
        there = me
        for bit, step in zip(bits, steps):
            if isinstance(bit, int):
                there = there + step if bit else there
            else:
                there = there + bit * step
        return there

    def of_chunk(c, work):
        for j in range(group):
            if j == 0:
                @pl.when(c > 0)
                def _():
                    work(c * group + j, partner(c, j))
            else:
                work(c * group + j, partner(c, j))

    def loop(start, stop, body):
        def step(c, carry):
            body(c)
            return carry

        lax.fori_loop(start, stop, step, 0)

    def each(work):
        loop(0, chunks, lambda c: of_chunk(c, work))

    def part(c):
        return pl.ds(pl.multiple_of(c * chunk, chunk), chunk)

    def rows_at(p):
        return pl.ds(pl.multiple_of(p * CAP, CAP), CAP)

    def pair(c):
        return pl.ds(pl.multiple_of(c * 2 * chunk, 2 * chunk), 2 * chunk)

    def home(p, whose):
        c, j = lax.div(p, group), lax.rem(p, group)
        return pl.ds(pl.multiple_of((c * 2 + whose) * chunk + j * CAP, CAP), CAP)

    def ask(p, there):
        return pltpu.make_async_remote_copy(
            src_ref=req.at[p], dst_ref=want.at[p], send_sem=rq_s.at[p],
            recv_sem=rq_r.at[p], device_id=(there, core), device_id_type=MESH)

    def fetch(p, there):
        return pltpu.make_async_remote_copy(
            src_ref=send.at[rows_at(p)], dst_ref=got.at[rows_at(p)], send_sem=f_s.at[p],
            recv_sem=f_r.at[p], device_id=(there, core), device_id_type=MESH)

    def give(p, there, side):
        return pltpu.make_async_remote_copy(
            src_ref=send.at[rows_at(p), pl.ds(pl.multiple_of(side * cut, cut), cut)],
            dst_ref=ret.at[home(p, core)], send_sem=r_s.at[side, p],
            recv_sem=r_r.at[core, p], device_id=(there, side), device_id_type=MESH)

    def given(p, whose):
        return pltpu.make_async_remote_copy(
            src_ref=ret.at[home(p, whose)], dst_ref=ret.at[home(p, whose)],
            send_sem=r_s.at[whose, p], recv_sem=r_r.at[whose, p],
            device_id=(me, 1 - core), device_id_type=MESH)

    def pass_row(whose):
        return pltpu.make_async_remote_copy(
            src_ref=wrow.at[whose], dst_ref=wrow.at[whose], send_sem=wx_s, recv_sem=wx_r,
            device_id=(me, 1 - core), device_id_type=MESH)

    loads = [
        pltpu.make_async_copy(src, dst, load_s.at[k])
        for k, (src, dst) in enumerate([(pas_hbm, pas), (q_hbm, q), (pos_hbm, pos)])
    ]

    barrier = pltpu.get_barrier_semaphore()
    each(lambda p, there: pl.semaphore_signal(
        barrier, inc=1, device_id=(there, core), device_id_type=MESH))
    pl.semaphore_signal(barrier, inc=1, device_id=(me, 1 - core), device_id_type=MESH)
    for load in loads:
        load.start()
    table = request_table(ids_ref[...], me, n, shard_rows)
    for p in range(n):
        req[p] = table[p : p + 1]
    want[0] = table[0:1]
    pl.semaphore_wait(barrier, n)

    each(lambda p, there: ask(p, there).start())

    def columns(rows, into, change):
        rows_t = turned(rows)
        for p in range(n):
            into[p * CAP : (p + 1) * CAP, :] = jnp.broadcast_to(
                change(rows_t[:CAP, p : p + 1]), (CAP, LANES))

    loads[0].wait()

    def gather(c):
        asked = turned(want[pl.ds(c * group, group), 0, :])
        w = jnp.concatenate(
            [jnp.broadcast_to(asked[:CAP, j : j + 1], (CAP, LANES)) for j in range(group)],
            axis=0)
        lane = iota((chunk, LANES), 1)
        hot = jnp.concatenate(
            [jnp.where(w == lane + k, 1.0, 0.0).astype(jnp.bfloat16)
             for k in range(0, shard_rows, LANES)], axis=1)
        send[part(c), :] = dot(hot, pas[...]).astype(jnp.bfloat16)

    def gather_and_send(c):
        of_chunk(c, lambda p, there: ask(p, there).wait_recv())
        gather(c)
        of_chunk(c, lambda p, there: fetch(p, there).start())

    def turned_by_core(i):
        return lax.rem(i + core * (chunks // 2), chunks)

    loop(0, chunks, lambda i: gather_and_send(turned_by_core(i)))
    got[0:CAP, :] = send[0:CAP, :]

    block = min(256, queries)
    wide = min(512, queries)

    def block_at(b):
        return pl.ds(pl.multiple_of(b * block, block), block)

    def other_form():
        wrow[core] = slot_row(want[:, 0, :], n)

    def mask():
        columns(req[:, 0, :], bias, lambda x: jnp.where(x >= 0, 0.0, NONE))

    def positive(b):
        both = q[block_at(b), :].astype(jnp.float32) * pos[block_at(b), :].astype(jnp.float32)
        total = both[:, :LANES]
        for k in range(LANES, depth, LANES):
            total = total + both[:, k : k + LANES]
        prow[:, block_at(b)] = scale * jnp.sum(total.T, axis=0, keepdims=True)

    def turn(b):
        wt[0:depth, block_at(b)] = q[block_at(b), :].T

    other_form()
    pass_row(core).start()
    mask()
    loads[1].wait()
    loads[2].wait()
    loop(0, queries // block, positive)
    loop(0, queries // block, turn)
    each(lambda p, there: ask(p, there).wait_send())

    power = scale * math.log2(math.e)

    def logits(c):
        def product(at):
            return dot(got[part(c), :], wt[0:depth, at : at + wide])

        ahead = product(0)
        for at in range(0, queries, wide):
            x = ahead
            if at + wide < queries:
                ahead = product(at + wide)
            x = x + jnp.concatenate([bias[part(c), :]] * (wide // LANES), axis=1)
            top = jnp.max(x, axis=0, keepdims=True)
            x = jnp.exp2(power * (x - top))
            big[part(c), at : at + wide] = x
            tops[c, :, at : at + wide] = scale * top
            sums[c, :, at : at + wide] = jnp.sum(x, axis=0, keepdims=True)

    def receive(c):
        of_chunk(c, lambda p, there: fetch(p, there).wait_recv())

        logits(c)

    loop(0, chunks, lambda i: receive(turned_by_core(i)))

    def totals():
        pos_logit = prow[...]
        top = pos_logit
        for c in range(chunks):
            top = jnp.maximum(top, tops[c])
        pos_exp = jnp.exp(pos_logit - top)
        total = pos_exp
        for c in range(chunks):
            total = total + sums[c] * jnp.exp(tops[c] - top)
        for c in range(chunks):
            tops[c] = jnp.exp(tops[c] - top) * (factor / total)
        crow[...] = factor * (pos_exp / total - 1.0)
        loss_ref[...] = top + jnp.log(total) - pos_logit

    totals()

    def row_grads(c):
        wt[part(c), :] = (big[part(c), :] * tops[c]).astype(jnp.bfloat16)
        send[part(c), :] = dot(wt[part(c), :], q[...]).astype(jnp.bfloat16)

    def return_rows(c):
        of_chunk(c, lambda p, there: fetch(p, there).wait_send())
        row_grads(c)

        @pl.when(c == 0)
        def _():
            give(0, me, 1 - core).start()

        def both(p, there):
            give(p, there, 0).start()
            give(p, there, 1).start()

        of_chunk(c, both)

    def wide_at(b):
        return pl.ds(pl.multiple_of(b * wide, wide), wide)

    def query_grads(b):
        g = dot(wt[:, wide_at(b)], got[...], ((0,), (0,)))
        coef = jnp.broadcast_to(crow[:, wide_at(b)], (LANES, wide)).T
        coef = jnp.concatenate([coef] * (depth // LANES), axis=1)
        g = g + coef * pos[wide_at(b), :].astype(jnp.float32)
        pas[wide_at(b), :] = g.astype(jnp.bfloat16)

    tall = min(512, shard_rows)

    def tall_at(b):
        return pl.ds(pl.multiple_of(b * tall, tall), tall)

    def clear(b):
        big[tall_at(b), 0:cut] = jnp.zeros((tall, cut), jnp.float32)

    loop(0, chunks, return_rows)
    mine = pl.ds(pl.multiple_of(core * cut, cut), cut)
    ret[home(0, core), :] = send[0:CAP, mine]
    loop(0, queries // wide, query_grads)
    pl.semaphore_signal(free_s, inc=1, device_id=(me, 1 - core), device_id_type=MESH)
    loop(0, shard_rows // tall, clear)
    pass_row(1 - core).wait_recv()

    def added(c, b):
        here = iota((tall, chunk), 0) + b * tall
        hot = jnp.concatenate(
            [jnp.where(here == wrow[whose, :, part(c)], 1.0, 0.0).astype(jnp.bfloat16)
             for whose in range(2)], axis=1)
        return big[tall_at(b), 0:cut] + dot(hot, ret[pair(c), :])

    def add_up(c):
        for b in range(shard_rows // tall):
            big[tall_at(b), 0:cut] = added(c, b)

    def add_last(b):
        pos[tall_at(b), mine] = added(chunks - 1, b).astype(jnp.bfloat16)

    def swap(b, side):
        block = pos.at[tall_at(b), pl.ds(pl.multiple_of(side * cut, cut), cut)]
        return pltpu.make_async_remote_copy(
            src_ref=block, dst_ref=block, send_sem=sw_s.at[b], recv_sem=sw_r.at[b],
            device_id=(me, 1 - core), device_id_type=MESH)

    def take(c):
        def both(p, there):
            given(p, 0).wait_recv()
            given(p, 1).wait_recv()

        of_chunk(c, both)

    def collect(c):
        take(c)
        add_up(c)

    given(0, 1 - core).wait_recv()
    loop(0, chunks - 1, collect)
    take(chunks - 1)
    pl.semaphore_wait(free_s, 1)
    for b in range(shard_rows // tall):
        add_last(b)
        swap(b, core).start()

    def sent(p, there):
        give(p, there, 0).wait_send()
        give(p, there, 1).wait_send()

    each(sent)
    give(0, me, 1 - core).wait_send()
    pass_row(core).wait_send()
    for b in range(shard_rows // tall):
        swap(b, core).wait_send()
        swap(b, 1 - core).wait_recv()


def hand_over(loss, grad_q, grad_p, loss_out, grad_q_out, grad_p_out, done):
    moves = [
        pltpu.make_async_copy(src, dst, done.at[k])
        for k, (src, dst) in enumerate(
            [(grad_p, grad_p_out), (grad_q, grad_q_out), (loss, loss_out)])
    ]
    for move in moves:
        move.start()
    for move in moves:
        move.wait()


def local(group, queries, positives, passages, negatives):
    n = lax.axis_size("idx")
    count, depth = queries.shape
    shard_rows = passages.shape[0]
    slots = n * CAP
    chunks = n // group
    any_space = pl.BlockSpec(memory_space=pl.ANY)
    vmem = pl.BlockSpec(memory_space=pltpu.VMEM)
    dma = pltpu.SemaphoreType.DMA
    bf16, f32 = jnp.bfloat16, jnp.float32
    loss, grad_q, grad_p = pl.pallas_call(
        functools.partial(kernel, n, group),
        out_shape=(
            pltpu.VMEM((1, count), f32),
            pltpu.VMEM((count, depth), bf16),
            pltpu.VMEM((shard_rows, depth), bf16),
        ),
        in_specs=[vmem, any_space, any_space, any_space],
        out_specs=(vmem, vmem, vmem),
        scratch_shapes=[
            pltpu.VMEM((count, depth), bf16),
            pltpu.VMEM((slots, depth), bf16),
            pltpu.VMEM((slots, depth), bf16),
            pltpu.VMEM((2 * slots, depth // 2), bf16),
            pltpu.VMEM((slots, count), f32),
            pltpu.VMEM((slots, count), bf16),
            pltpu.VMEM((n, 1, LANES), jnp.int32),
            pltpu.VMEM((n, 1, LANES), jnp.int32),
            pltpu.VMEM((slots, LANES), f32),
            pltpu.VMEM((2, 1, slots), jnp.int32),
            pltpu.VMEM((chunks, 1, count), f32),
            pltpu.VMEM((chunks, 1, count), f32),
            pltpu.VMEM((1, count), f32),
            pltpu.VMEM((1, count), f32),
            dma((3,)),
            dma((n,)), dma((n,)),
            dma((n,)), dma((n,)),
            dma((2, n)), dma((2, n)),
            dma, dma,
            dma((shard_rows // min(512, shard_rows),)),
            dma((shard_rows // min(512, shard_rows),)),
            pltpu.SemaphoreType.REGULAR,
        ],
        compiler_params=pltpu.CompilerParams(
            collective_id=0, has_side_effects=True, vmem_limit_bytes=52 << 20
        ),
        cost_estimate=pl.CostEstimate(
            flops=12 * slots * count * depth, bytes_accessed=20 * count * depth,
            transcendentals=slots * count,
        ),
    )(negatives.reshape(1, -1), queries, positives, passages)
    loss, grad_q, grad_p = pl.pallas_call(
        hand_over,
        out_shape=(
            jax.ShapeDtypeStruct((1, count), f32),
            jax.ShapeDtypeStruct((count, depth), bf16),
            jax.ShapeDtypeStruct((shard_rows, depth), bf16),
        ),
        in_specs=[any_space] * 3,
        out_specs=(any_space,) * 3,
        scratch_shapes=[dma((3,))],
        compiler_params=pltpu.CompilerParams(vmem_limit_bytes=1 << 20),
    )(loss, grad_q, grad_p)
    return loss.reshape(-1), grad_q, grad_p


def solution(mesh, group=8):
    placed = (
        P(("idx", "enc"), None),
        P(("idx", "enc"), None),
        P("idx", None),
        P(("idx", "enc"), None),
    )
    return jax.shard_map(
        functools.partial(local, group),
        mesh=mesh,
        in_specs=placed,
        out_specs=(P(("idx", "enc")), P(("idx", "enc"), None), P("idx", None)),
        check_vma=False,
    )
```
